256 devices in a mesh: pa: 32 (over x, y, core), ch: 8 (over z).
Axes of the slice: x: 4, y: 4, z: 8, core: 2. Of those that a mesh axis runs over, the one named last changes fastest.
Arguments:
- basis_prev: float32 [64, 48, 4, 2048], P('pa', None, None, 'ch')
- basis_now: float32 [64, 48, 4, 2048], P('pa', None, None, 'ch')
- beta_prev: float32 [4], replicated, may hold values from 0.3 to 0.9
- propagator: float32 [64, 48, 4], P('pa'), may hold values from 0.3 to 1
- spline: bfloat16 [32, 32, 4, 48, 16], P(None, 'pa'), may hold values from -0.25 to 0.25
- coupling: bfloat16 [3, 2048, 2048], P(None, None, 'ch'), as said below
- edge_offset: int32 [32, 32, 4], replicated, may hold values from 0 to 80
- edge_tile: int32 [32, 32, 4], replicated, may hold values from 0 to 1
- edge_term: int32 [32, 32, 4], replicated, may hold values from 0 to 2
- edge_count: int32 [32, 32], replicated, may hold values from 0 to 4, as said below
Outputs:
- basis_next: float32 [64, 48, 4, 2048], P('pa', None, None, 'ch')
- coefficients: float32 [4, 4], replicated
The draws below stay inside these ranges and needn't reach their ends.
Inputs may be any that keep to these rules, and one draw needn't show every extreme that they name: `edge_count`: in every draw some target interval has all 4 slots live from every source interval. Each of the 3 coupling matrices is symmetric.
All inputs are finite; a program needn't handle non-finite values.
Results may differ from the reference program's by a relative error of at most 0.006.
Values may be sent and summed in bfloat16 or wider, within the bound.
A program may use at most 64 MiB of HBM per device.

```python
import math
import jax
import jax.numpy as jnp
from jax import lax

NP = 64
NQ = 48
NCH = 2048
NE = 4
TERMS = 3
SUP = 16
SLOT = 4
ITERS = 2
NPI = 32
P_DEV = 2
SRC_PTS = 96
CH_LOC = 256


def amplitude_scales(key):
    key_row, key_col = jax.random.split(key)
    row_scale = 10.0 ** jax.random.uniform(key_row, (NP, NQ, 1, 1), jnp.float32)
    col_scale = 10.0 ** jax.random.uniform(key_col, (1, 1, NE, NCH), jnp.float32)
    mean_square = (10.0 ** 2.0 - 1.0) / (2.0 * math.log(10.0))
    rising = 3.0 ** (jnp.arange(NP, dtype=jnp.float32) / (NP - 1))
    return row_scale * col_scale * rising[:, None, None, None] / (mean_square * 2.0)


def draw_basis_prev(key, part):
    key = jax.random.fold_in(key, 11)
    key_scale, key_value = jax.random.split(key)
    values = jax.random.normal(key_value, (NP, NQ, NE, NCH), jnp.float32)
    return (values * amplitude_scales(key_scale)).astype(jnp.float32)


def draw_basis_now(key, part):
    key = jax.random.fold_in(key, 12)
    key_scale, key_value = jax.random.split(key)
    values = jax.random.normal(key_value, (NP, NQ, NE, NCH), jnp.float32)
    return (values * amplitude_scales(key_scale)).astype(jnp.float32)


def group_factors(key):
    key_order, key_jitter = jax.random.split(key)
    groups = NCH // CH_LOC
    order = jax.random.permutation(key_order, groups).astype(jnp.float32)
    jitter = jax.random.uniform(key_jitter, (groups,), jnp.float32)
    exponent = (order + jitter) / groups - 0.5
    mean_square = (10.0 - 0.1) / (2.0 * math.log(10.0))
    scales = 10.0 ** exponent / mean_square ** 0.5
    return jnp.repeat(scales, CH_LOC, total_repeat_length=NCH)


def draw_coupling(key, part):
    key = jax.random.fold_in(key, 13)
    key_base, key_group = jax.random.split(key)
    base = jax.random.normal(key_base, (TERMS, NCH, NCH), jnp.float32)
    symmetric = (base + jnp.swapaxes(base, 1, 2)) * 0.5 ** 0.5 / NCH ** 0.5
    channel_scale = group_factors(key_group)
    scaled = symmetric * channel_scale[None, :, None] * channel_scale[None, None, :]
    return scaled.astype(jnp.bfloat16)


def draw_edge_count(key, part):
    key = jax.random.fold_in(key, 17)
    key_counts, key_full = jax.random.split(key)
    counts = jax.random.randint(key_counts, (NPI, NPI), 0, SLOT + 1, jnp.int32)
    full_target = jax.random.randint(key_full, (), 0, NPI, jnp.int32)
    columns = jnp.arange(NPI, dtype=jnp.int32)[None, :]
    return jnp.where(columns == full_target, SLOT, counts).astype(jnp.int32)


def place_ends(values, own_key, smallest, top_value):
    index_at = [jax.random.randint(jax.random.fold_in(own_key, axis), (), 0, length) for axis, length in enumerate(values.shape)]
    main_axis = values.shape.index(max(values.shape))
    beside = index_at[:main_axis] + [(index_at[main_axis] + 1) % values.shape[main_axis]] + index_at[main_axis + 1:]
    return values.at[tuple(index_at)].set(smallest).at[tuple(beside)].set(top_value)


def block_levels(rng, extent, cuts, least, high):
    def one(axis_at, parts):
        draws = jax.random.uniform(jax.random.fold_in(jax.random.fold_in(rng, 6), axis_at), (parts,), jnp.float32, least / len(cuts), high / len(cuts))
        return jnp.repeat(jnp.exp(draws), extent[axis_at] // parts).reshape((-1,) + (1,) * (len(extent) - axis_at - 1))

    factor_of = one(*cuts[0])
    for cut in cuts[1:]:
        factor_of = factor_of * one(*cut)
    return factor_of


def normal_values(rng, extent, deviation, limit, cuts=(), held_as=jnp.bfloat16):
    gain = block_levels(rng, extent, cuts, -0.22, 0.18) if cuts else 1.0
    entries = jax.random.normal(rng, extent, jnp.float32) * deviation * gain
    return jnp.minimum(jnp.maximum(entries, -limit), limit).astype(held_as)


def setup_inputs(seed: int = 0) -> dict:
    splits = jax.random.split(jax.random.key(seed), 11)
    basis_prev = draw_basis_prev(jax.random.fold_in(splits[10], 71), 0)
    basis_now = draw_basis_now(jax.random.fold_in(splits[10], 71), 0)
    beta_prev = jnp.clip(jnp.exp(jax.random.uniform(splits[2], (NE,), jnp.float32, math.log(0.3), math.log(0.9))), 0.3, 0.9)
    propagator = jnp.clip(0.3 + 0.7 * jax.random.uniform(splits[3], (NP, NQ, NE), jnp.float32) ** block_levels(splits[3], (NP, NQ, NE), ((0, 32),), -0.2, 0.2), 0.3, 1.0)
    spline = normal_values(splits[4], (NPI, NPI, SLOT, NQ, SUP), (NPI * SLOT * SUP // (2 * P_DEV)) ** -0.5, 0.25, ((1, 32),))
    coupling = draw_coupling(jax.random.fold_in(splits[10], 71), 0)
    edge_offset = place_ends(jax.random.randint(splits[6], (NPI, NPI, SLOT), 0, SRC_PTS - SUP + 1), jax.random.fold_in(splits[6], 1), 0, SRC_PTS - SUP).astype(jnp.int32)
    edge_tile = place_ends(jax.random.randint(splits[7], (NPI, NPI, SLOT), 0, P_DEV), jax.random.fold_in(splits[7], 1), 0, P_DEV - 1).astype(jnp.int32)
    edge_term = place_ends(jax.random.randint(splits[8], (NPI, NPI, SLOT), 0, TERMS), jax.random.fold_in(splits[8], 1), 0, TERMS - 1).astype(jnp.int32)
    edge_count = draw_edge_count(jax.random.fold_in(splits[10], 71), 0)
    return dict(basis_prev=basis_prev, basis_now=basis_now, beta_prev=beta_prev, propagator=propagator, spline=spline, coupling=coupling, edge_offset=edge_offset, edge_tile=edge_tile, edge_term=edge_term, edge_count=edge_count)


def permute(amplitude, spline, coupling, edge_offset, edge_tile, edge_term, edge_count):
    flat_field = amplitude.astype(jnp.float32).reshape(NPI, SRC_PTS, NE * NCH)
    source_ids = jnp.arange(NPI, dtype=jnp.int32)[:, None, None]

    def one_target(target):
        offsets = edge_offset[:, target, :]
        indices = offsets[:, :, None] + jnp.arange(SUP, dtype=jnp.int32)[None, None, :]
        support_rows = flat_field[source_ids, indices]
        live_slots = (jnp.arange(SLOT, dtype=jnp.int32)[None, :] < edge_count[:, target][:, None]).astype(jnp.float32)
        weights = spline[:, target].astype(jnp.float32) * live_slots[:, :, None, None]
        products = jnp.einsum('slqj,sljc->slqc', weights, support_rows)
        term_hit = edge_term[:, target][:, :, None] == jnp.arange(TERMS, dtype=jnp.int32)[None, None, :]
        tile_hit = edge_tile[:, target][:, :, None] == jnp.arange(P_DEV, dtype=jnp.int32)[None, None, :]
        selector = (term_hit[:, :, :, None] & tile_hit[:, :, None, :]).astype(jnp.float32)
        interpolated = jnp.einsum('slkt,slqc->ktqc', selector, products)
        return interpolated.astype(jnp.bfloat16)
    stacked = lax.map(one_target, jnp.arange(NPI, dtype=jnp.int32))
    stacked = jnp.transpose(stacked, (1, 0, 2, 3, 4)).reshape(TERMS, NP * NQ * NE, NCH)
    permuted = jnp.zeros((NP * NQ * NE, NCH), jnp.float32)
    for term_index in range(TERMS):
        permuted = permuted + jnp.dot(stacked[term_index].astype(jnp.float32), coupling[term_index].astype(jnp.float32))
    return permuted.reshape(NP, NQ, NE, NCH)

def reference(basis_prev, basis_now, beta_prev, propagator, spline, coupling, edge_offset, edge_tile, edge_term, edge_count):
    cell_count = float(NP * NQ * NCH)
    basis_old, basis_cur, beta_old = (basis_prev, basis_now, beta_prev)
    coefficients = []
    for iteration in range(ITERS):
        image = permute(basis_cur.astype(jnp.bfloat16), spline, coupling, edge_offset, edge_tile, edge_term, edge_count)
        applied = basis_cur - propagator[..., None] * image
        alpha_now = lax.optimization_barrier(jnp.sum(basis_cur * applied, axis=(0, 1, 3))) / cell_count
        residual = applied - alpha_now[:, None] * basis_cur - beta_old[:, None] * basis_old
        beta_now = jnp.sqrt(lax.optimization_barrier(jnp.sum(residual * residual, axis=(0, 1, 3))) / cell_count + 1e-06)
        basis_old, basis_cur, beta_old = (basis_cur, residual / beta_now[:, None], beta_now)
        coefficients.append(alpha_now)
        coefficients.append(beta_now)
    return (basis_cur, jnp.stack(coefficients))
```

```python
import jax
import jax.numpy as jnp
from jax import lax
from jax.experimental import pallas as pl
from jax.experimental.pallas import tpu as pltpu
from jax.sharding import PartitionSpec as P

MESH = pl.DeviceIdType.MESH
EPS = 1e-06
ROWS = 96
HALF = 48
CH = 256
CELLS = 6291456.0


def shifted(position):
    c = position % 2
    y = (position // 2) % 4
    return position // 8, (y - c + 4) % 4, c


def place(x, yp, c):
    return (x * 4 + (yp + c) % 4) * 2 + c


def energy_of(t, g):
    return (t % 2) * 2 + 1 - (t // 2 + g) % 2


def kernel(
    q1_in,
    q0_in,
    beta_in,
    prop_in,
    sp_in,
    meta_in,
    cpl,
    out,
    coef,
    xs,
    spg,
    dmat,
    xg,
    acc,
    u2,
    pbuf,
    rs_s,
    rs_r,
    q1g,
    q0g,
    pg,
    y1g,
    sg,
    q2g,
    s2g,
    fin_q,
    fin_s,
    redv,
    red_a,
    redt,
    red_b,
    coefg,
    sem_x,
    sem_in,
    sem_ag,
    sem_rs,
    sem_ra,
    sem_rb,
    sem_fin,
):
    pa = lax.axis_index("pa")
    z = lax.axis_index("ch")
    X, yp, c = shifted(pa)
    g = yp // 2
    th = yp % 2
    tme = th * 2 + c
    a = 1 - (th + g) % 2
    e = c * 2 + a
    j = X * 2 + g
    f32 = jnp.float32
    bf16 = jnp.bfloat16

    def member(t):
        return (place(X, 2 * g + t // 2, t % 2), z)

    def peer(jj):
        gg = jj % 2
        return (place(jj // 2, 2 * gg + (gg + 1 - a) % 2, c), z)

    others = [(tme + d) % 4 for d in range(1, 4)]
    peers = [(j + d) % 8 for d in range(1, 8)]
    zs = [(z + d) % 8 for d in range(1, 8)]

    barrier = pltpu.get_barrier_semaphore()
    friends = [member(t) for t in others] + [peer(p) for p in peers] + [(pa, q) for q in zs]
    for d in friends:
        pl.semaphore_signal(barrier, inc=1, device_id=d, device_id_type=MESH)
    pl.semaphore_wait(barrier, len(friends))

    def remote(src, dst, send, recv, device):
        return pltpu.make_async_remote_copy(
            src_ref=src, dst_ref=dst, send_sem=send, recv_sem=recv, device_id=device, device_id_type=MESH
        )

    def x_copy(d, slot):
        t = others[d]
        return remote(xs.at[d], xg.at[0, slot, j], sem_x.at[0, d], sem_x.at[1, slot], member(t))

    def in_copy(kind, d, slot):
        t = others[d]
        em = energy_of(t, g)
        src = (sp_in, q1_in.at[em], q0_in.at[em], prop_in.at[em])[kind]
        dst = (spg, q1g, q0g, pg)[kind].at[slot]
        return remote(src, dst, sem_in.at[0, kind, d], sem_in.at[1, kind, slot], member(t))

    for d in range(3):
        xs[d] = q1_in[energy_of(others[d], g)].astype(bf16)
        x_copy(d, tme).start()
    for d in range(3):
        in_copy(0, d, tme).start()
    xg[0, tme, j] = q1_in[e].astype(bf16)
    spg[tme] = sp_in[...]
    q1g[tme] = q1_in[e]
    q0g[tme] = q0_in[e]
    pg[tme] = prop_in[e]

    xr, xl, xo = (X + 1) % 4, (X + 3) % 4, (X + 2) % 4
    dev_r, dev_l = peer(xr * 2 + g), peer(xl * 2 + g)
    dev_p = peer(X * 2 + 1 - g)

    def ag_ref(it, t, slot, part):
        if part is None:
            return xg.at[it, t, slot]
        return xg.at[it, t, slot, pl.ds(part * HALF, HALF)]

    def ag_send(it, t, k):
        slot, part, dev = (
            (j, None, dev_r),
            (j, None, dev_l),
            (xl * 2 + g, 0, dev_r),
            (xr * 2 + g, 1, dev_l),
            (j, None, dev_p),
            (xl * 2 + g, None, dev_p),
            (xr * 2 + g, None, dev_p),
            (xo * 2 + g, 0, dev_p),
            (xo * 2 + g, 1, dev_p),
        )[k]
        ref = ag_ref(it, t, slot, part)
        return remote(ref, ref, sem_ag.at[it, 0, t, k], sem_ag.at[it, 1, t, k], dev)

    def ag_recv(it, t, k):
        h = 1 - g
        slot, part = (
            (xl * 2 + g, None),
            (xr * 2 + g, None),
            (xo * 2 + g, 0),
            (xo * 2 + g, 1),
            (X * 2 + h, None),
            (xl * 2 + h, None),
            (xr * 2 + h, None),
            (xo * 2 + h, 0),
            (xo * 2 + h, 1),
        )[k]
        ref = ag_ref(it, t, slot, part)
        remote(ref, ref, sem_ag.at[it, 0, t, k], sem_ag.at[it, 1, t, k], dev_p).wait_recv()

    def ag_first(it, t):
        for k in (0, 1, 4):
            ag_send(it, t, k).start()

    def ag_second(it, t):
        ag_recv(it, t, 0)
        ag_send(it, t, 2).start()
        ag_send(it, t, 5).start()
        ag_recv(it, t, 1)
        ag_send(it, t, 3).start()
        ag_send(it, t, 6).start()

    def ag_third(it, t):
        for k in (2, 3):
            ag_recv(it, t, k)
            ag_send(it, t, k + 5).start()

    def ag_last(it, t):
        for k in (4, 5, 6, 7, 8):
            ag_recv(it, t, k)

    row_ids = lax.broadcasted_iota(jnp.int32, (4 * ROWS, CH), 0)

    def build(tt):
        def one(ts, carry):
            for half in range(2):
                b = ts * 2 + half
                meta = meta_in[tt, b]
                key = lax.shift_right_logical(meta, 10)
                row = meta & 1023
                tile = spg[tt, b]
                parts = []
                for kt in range(6):
                    mask = jnp.where(key == kt, 1.0, 0.0).astype(bf16)
                    parts.append(tile * mask)
                weights = jnp.concatenate(parts, axis=0)
                hot = jnp.where(row_ids == row, 1.0, 0.0).astype(bf16)
                block = lax.dot_general(weights, hot, (((1,), (1,)), ((), ())), preferred_element_type=f32)
                dmat[ts, tt, :, half * 384 : half * 384 + 384] = block.astype(bf16)
            return carry

        lax.fori_loop(0, 4, one, 0)

    def spline_step(it, ts, first, last):
        def one(tt, carry):
            field = xg[it, ts].reshape(8 * ROWS, CH)
            part = jnp.dot(dmat[ts, tt], field, preferred_element_type=f32)
            if not first:
                part = acc[tt] + part
            if last:
                for k in range(3):
                    u2[tt, :, k * CH : (k + 1) * CH] = part[k * ROWS : (k + 1) * ROWS].astype(bf16)
            else:
                acc[tt] = part
            return carry

        lax.fori_loop(0, 4, one, 0)

    def couple(r):
        dest = (z + r) % 8
        rows = pl.ds(pl.multiple_of(dest * CH, CH), CH)
        total = None
        for k in range(3):
            left = u2[:, :, k * CH : (k + 1) * CH].reshape(4 * ROWS, CH)
            part = lax.dot_general(left, cpl[k, rows, :], (((1,), (1,)), ((), ())), preferred_element_type=f32)
            total = part if total is None else total + part
        pbuf[r] = total.reshape(4, ROWS, CH)

    z_dev = ((pa, (z + 1) % 8), (pa, (z + 7) % 8))

    def rs_copy(it, way, step, t):
        if step == 0:
            src = rs_s.at[it, way, 0, t, pl.ds(way * HALF, HALF)]
            dst = rs_r.at[it, way, 0, t, pl.ds(way * HALF, HALF)]
        else:
            src = rs_s.at[it, way, step, t]
            dst = rs_r.at[it, way, step, t]
        return remote(src, dst, sem_rs.at[it, 0, way, step, t], sem_rs.at[it, 1, way, step, t], z_dev[way])

    def rs_begin(it):
        couple(4)

        def one(t, carry):
            for way in range(2):
                lo = way * HALF
                rs_s[it, way, 0, t, lo : lo + HALF] = pbuf[4, t, lo : lo + HALF].astype(bf16)
                rs_copy(it, way, 0, t).start()
            return carry

        lax.fori_loop(0, 4, one, 0)

    def rs_step(it, step):
        rel = (4 - step, 4 + step)
        couple(rel[0])
        couple(rel[1])

        def one(t, carry):
            for way in range(2):
                rs_copy(it, way, step - 1, t).wait_recv()
                if step == 1:
                    lo = way * HALF
                    hi = HALF - lo
                    rs_s[it, way, 1, t, lo : lo + HALF] = (
                        pbuf[rel[way], t, lo : lo + HALF] + rs_r[it, way, 0, t, lo : lo + HALF].astype(f32)
                    ).astype(bf16)
                    rs_s[it, way, 1, t, hi : hi + HALF] = pbuf[rel[way], t, hi : hi + HALF].astype(bf16)
                else:
                    rs_s[it, way, step, t] = (
                        pbuf[rel[way], t] + rs_r[it, way, step - 1, t].astype(f32)
                    ).astype(bf16)
                rs_copy(it, way, step, t).start()
            return carry

        lax.fori_loop(0, 4, one, 0)

    def rs_end(it, t):
        for way in range(2):
            rs_copy(it, way, 3, t).wait_recv()
        return pbuf[0, t] + (rs_r[it, 0, 3, t].astype(f32) + rs_r[it, 1, 3, t].astype(f32))

    def fold(it, row, value):
        line = jnp.sum(value, axis=0, keepdims=True)
        redv[it, row : row + 1, :] += line[:, :128] + line[:, 128:]

    def ra_copy(it, q, slot):
        return remote(redv.at[it], red_a.at[it, slot], sem_ra.at[it, 0, q], sem_ra.at[it, 1, slot], (pa, q))

    def rb_copy(it, p, slot):
        return remote(redt.at[it], red_b.at[it, slot], sem_rb.at[it, 0, p], sem_rb.at[it, 1, slot], peer(p))

    def reduce_first(it):
        red_a[it, z] = redv[it]
        for q in zs:
            ra_copy(it, q, z).start()

    def reduce_second(it):
        for q in zs:
            ra_copy(it, q, q).wait_recv()
        total = red_a[it, 0]
        for i in range(1, 8):
            total = total + red_a[it, i]
        redt[it] = total
        red_b[it, j] = total
        for p in peers:
            rb_copy(it, p, j).start()

    def reduce_last(it):
        for p in peers:
            rb_copy(it, p, p).wait_recv()
        total = red_b[it, 0]
        for i in range(1, 8):
            total = total + red_b[it, i]
        sums = jnp.sum(total, axis=1, keepdims=True)
        qw, ss, sq, qq = sums[0:1], sums[1:2], sums[2:3], sums[3:4]
        alpha = qw / CELLS
        rest = 1.0 - alpha
        squares = ss + 2.0 * rest * sq + rest * rest * qq
        beta = jnp.sqrt(jnp.maximum(squares, 0.0) / CELLS + EPS)
        return alpha, rest, beta

    redv[...] = jnp.zeros_like(redv)
    ag_first(0, tme)
    for d in range(3):
        x_copy(d, others[d]).wait_recv()
        ag_first(0, others[d])
    build(tme)
    order = [tme] + others
    for t in order:
        ag_second(0, t)
    for kind in (1, 2, 3):
        for d in range(3):
            in_copy(kind, d, tme).start()
    for d in range(3):
        in_copy(0, d, others[d]).wait_recv()
        build(others[d])
        if d == 0:
            for t in order:
                ag_third(0, t)
    for t in range(4):
        ag_last(0, t)
        spline_step(0, t, t == 0, t == 3)
    rs_begin(0)
    for step in (1, 2, 3):
        rs_step(0, step)
    couple(0)
    for kind in (1, 2, 3):
        for d in range(3):
            in_copy(kind, d, others[d]).wait_recv()
    beta0 = beta_in[e][0:1, 0:1]

    def first_end(t):
        y = rs_end(0, t)
        y1g[t] = y
        q1 = q1g[t]
        pw = jnp.concatenate([pg[t], pg[t]], axis=1) * y
        s = -pw - beta0 * q0g[t]
        sg[t] = s
        xg[1, t, j] = s.astype(bf16)
        ag_first(1, t)
        fold(0, 0, q1 * (q1 - pw))
        fold(0, 1, s * s)
        fold(0, 2, s * q1)
        fold(0, 3, q1 * q1)

    first_end(0)
    first_end(1)
    ag_second(1, 0)
    first_end(2)
    ag_second(1, 1)
    ag_third(1, 0)
    first_end(3)
    reduce_first(0)

    ag_second(1, 2)
    ag_third(1, 1)
    ag_second(1, 3)
    ag_third(1, 2)
    ag_last(1, 0)
    spline_step(1, 0, True, False)
    reduce_second(0)
    ag_third(1, 3)
    for t in range(1, 4):
        ag_last(1, t)
        spline_step(1, t, False, t == 3)
    rs_begin(1)
    rs_step(1, 1)
    alpha1, rest1, beta1 = reduce_last(0)

    def fin_copy(kind, d, slot):
        t = others[d]
        src = (q2g.at[t], s2g.at[t], coefg.at[e])[kind]
        dst = (fin_q, fin_s, coefg)[kind].at[slot]
        return remote(src, dst, sem_fin.at[0, kind, d], sem_fin.at[1, kind, slot], member(t))

    for t in range(4):
        q2g[t] = (sg[t] + rest1 * q1g[t]) / beta1
    fin_q[e] = q2g[tme]
    for d in range(3):
        fin_copy(0, d, e).start()
    rs_step(1, 2)
    rs_step(1, 3)
    couple(0)
    for t in range(4):
        y = (rs_end(1, t) + rest1 * y1g[t]) / beta1
        q2 = q2g[t]
        pw = jnp.concatenate([pg[t], pg[t]], axis=1) * y
        s = -pw - beta1 * q1g[t]
        s2g[t] = s
        fold(1, 0, q2 * (q2 - pw))
        fold(1, 1, s * s)
        fold(1, 2, s * q2)
        fold(1, 3, q2 * q2)
    reduce_first(1)
    fin_s[e] = s2g[tme]
    for d in range(3):
        fin_copy(1, d, e).start()
    reduce_second(1)
    alpha2, rest2, beta2 = reduce_last(1)
    wide = lambda v: jnp.broadcast_to(v, (1, 128))
    coefg[e] = jnp.concatenate(
        [wide(alpha1), wide(beta1), wide(alpha2), wide(beta2), jnp.zeros((4, 128), f32)], axis=0
    )
    for d in range(3):
        fin_copy(2, d, e).start()
    for kind in range(3):
        for d in range(3):
            fin_copy(kind, d, energy_of(others[d], g)).wait_recv()
    lanes = lax.broadcasted_iota(jnp.int32, (8, 128), 1)
    table = jnp.zeros((8, 128), f32)
    for q in range(4):
        mine = coefg[q]
        table = jnp.where(lanes == q, mine, table)
        rest = 1.0 - mine[2:3, 0:1]
        out[q] = (fin_s[q] + rest * fin_q[q]) / mine[3:4, 0:1]
    coef[...] = table

    for d in range(3):
        x_copy(d, tme).wait_send()
        for kind in range(4):
            in_copy(kind, d, tme).wait_send()
        for kind in range(3):
            fin_copy(kind, d, e).wait_send()
    for it in range(2):

        def drain(t, carry):
            for k in range(9):
                ag_send(it, t, k).wait_send()
            for way in range(2):
                for step in range(4):
                    rs_copy(it, way, step, t).wait_send()
            return carry

        lax.fori_loop(0, 4, drain, 0)
        for q in zs:
            ra_copy(it, q, z).wait_send()
        for p in peers:
            rb_copy(it, p, j).wait_send()


def reorder(values):
    tail = values.shape[1:]
    values = values.reshape((4, 4, 2) + tail)
    values = jnp.stack([values[:, :, 0], jnp.roll(values[:, :, 1], -1, axis=1)], axis=2)
    values = values.reshape((2, 2, 2, 2, 2) + tail)
    rest = tuple(range(5, 5 + len(tail)))
    return values.transpose((3, 4, 0, 1, 2) + rest).reshape((8, 4) + tail)


def body(
    basis_prev,
    basis_now,
    beta_prev,
    propagator,
    spline,
    coupling,
    edge_offset,
    edge_tile,
    edge_term,
    edge_count,
):
    f32 = jnp.float32
    bf16 = jnp.bfloat16
    by_energy = lambda v: v.reshape(ROWS, 4, CH).transpose(1, 0, 2)
    q1 = by_energy(basis_now)
    q0 = by_energy(basis_prev)
    prop = jnp.broadcast_to(propagator.reshape(ROWS, 4).T[:, :, None], (4, ROWS, 128))
    beta = jnp.broadcast_to(beta_prev[:, None, None], (4, 8, 128))
    tiles = reorder(spline[:, 0])
    tiles = tiles.transpose(0, 3, 1, 2, 4).reshape(8, HALF, CH)

    X, yp, _ = shifted(lax.axis_index("pa"))
    targets = jnp.stack([place(X, 2 * (yp // 2) + t // 2, t % 2) for t in range(4)])
    live = jnp.arange(4, dtype=jnp.int32)[None, None, :] < edge_count[:, :, None]
    packed = jnp.where(live, edge_term * 2 + edge_tile, 6) * 1024 + edge_offset
    packed = reorder(jnp.take(packed, targets, axis=1))
    packed = packed.transpose(2, 0, 1, 3)[..., None]
    shift = (
        jnp.arange(4, dtype=jnp.int32)[:, None, None] * ROWS + jnp.arange(16, dtype=jnp.int32)[None, None, :]
    )
    meta = (packed + shift).reshape(4, 8, 1, CH)

    vmem = pl.BlockSpec(memory_space=pltpu.VMEM)
    dma = pltpu.SemaphoreType.DMA
    out, coef = pl.pallas_call(
        kernel,
        out_shape=(
            jax.ShapeDtypeStruct((4, ROWS, CH), f32),
            jax.ShapeDtypeStruct((8, 128), f32),
        ),
        in_specs=[vmem] * 7,
        out_specs=(vmem, vmem),
        scratch_shapes=[
            pltpu.VMEM((3, ROWS, CH), bf16),
            pltpu.VMEM((4, 8, HALF, CH), bf16),
            pltpu.VMEM((4, 4, 288, 768), bf16),
            pltpu.VMEM((2, 4, 8, ROWS, CH), bf16),
            pltpu.VMEM((4, 288, CH), f32),
            pltpu.VMEM((4, ROWS, 768), bf16),
            pltpu.VMEM((8, 4, ROWS, CH), f32),
            pltpu.VMEM((2, 2, 4, 4, ROWS, CH), bf16),
            pltpu.VMEM((2, 2, 4, 4, ROWS, CH), bf16),
            pltpu.VMEM((4, ROWS, CH), f32),
            pltpu.VMEM((4, ROWS, CH), f32),
            pltpu.VMEM((4, ROWS, 128), f32),
            pltpu.VMEM((4, ROWS, CH), f32),
            pltpu.VMEM((4, ROWS, CH), f32),
            pltpu.VMEM((4, ROWS, CH), f32),
            pltpu.VMEM((4, ROWS, CH), f32),
            pltpu.VMEM((4, ROWS, CH), f32),
            pltpu.VMEM((4, ROWS, CH), f32),
            pltpu.VMEM((2, 8, 128), f32),
            pltpu.VMEM((2, 8, 8, 128), f32),
            pltpu.VMEM((2, 8, 128), f32),
            pltpu.VMEM((2, 8, 8, 128), f32),
            pltpu.VMEM((4, 8, 128), f32),
            dma((2, 4)),
            dma((2, 4, 4)),
            dma((2, 2, 4, 9)),
            dma((2, 2, 2, 4, 4)),
            dma((2, 2, 8)),
            dma((2, 2, 8)),
            dma((2, 3, 4)),
        ],
        compiler_params=pltpu.CompilerParams(
            collective_id=0, has_side_effects=True, vmem_limit_bytes=56 * 1024 * 1024
        ),
    )(q1, q0, beta, prop, tiles, meta, coupling)
    basis_next = out.transpose(1, 0, 2).reshape(2, 48, 4, CH)
    return basis_next, coef[:4, :4]


def solution(mesh):
    placed = (
        P("pa", None, None, "ch"),
        P("pa", None, None, "ch"),
        P(),
        P("pa", None, None),
        P(None, "pa", None, None, None),
        P(None, None, "ch"),
        P(),
        P(),
        P(),
        P(),
    )
    return jax.shard_map(
        body,
        mesh=mesh,
        in_specs=placed,
        out_specs=(P("pa", None, None, "ch"), P()),
        check_vma=False,
    )
```

```python
import jax
import jax.numpy as jnp
from jax import lax
from jax.experimental import pallas as pl
from jax.experimental.pallas import tpu as pltpu
from jax.sharding import PartitionSpec as P

MESH = pl.DeviceIdType.MESH
EPS = 1e-06
ROWS = 96
HALF = 48
CH = 256
CELLS = 6291456.0


def shifted(position):
    c = position % 2
    y = (position // 2) % 4
    return position // 8, (y - c + 4) % 4, c


def place(x, yp, c):
    return (x * 4 + (yp + c) % 4) * 2 + c


def owned(position):
    _, yp, c = shifted(position)
    return energy_of((yp % 2) * 2 + c, yp // 2)


def energy_of(t, g):
    return (t % 2) * 2 + 1 - (t // 2 + g) % 2


def kernel(
    q1_in,
    q0_in,
    beta_in,
    prop_in,
    sp_in,
    meta_in,
    cpl,
    out,
    coef,
    xs,
    spg,
    dmat,
    xg,
    acc,
    u2,
    pbuf,
    rs_s,
    rs_r,
    q1g,
    q0g,
    pg,
    y1g,
    sg,
    q2g,
    s2g,
    fin_q,
    fin_s,
    redv,
    red_a,
    redt,
    red_b,
    red_c,
    sem_x,
    sem_in,
    sem_ag,
    sem_rs,
    sem_ra,
    sem_rb,
    sem_rc,
    sem_fin,
):
    pa = lax.axis_index("pa")
    z = lax.axis_index("ch")
    X, yp, c = shifted(pa)
    g = yp // 2
    th = yp % 2
    tme = th * 2 + c
    a = 1 - (th + g) % 2
    e = c * 2 + a
    j = X * 2 + g
    f32 = jnp.float32
    bf16 = jnp.bfloat16

    def member(t):
        return (place(X, 2 * g + t // 2, t % 2), z)

    def peer(jj):
        gg = jj % 2
        return (place(jj // 2, 2 * gg + (gg + 1 - a) % 2, c), z)

    others = [(tme + d) % 4 for d in range(1, 4)]
    peers = [(j + d) % 8 for d in range(1, 8)]
    plane = [(pa + d) % 32 for d in range(1, 32)]
    zs = [(z + d) % 8 for d in range(1, 8)]

    barrier = pltpu.get_barrier_semaphore()
    friends = [(q, z) for q in plane] + [(pa, q) for q in zs]
    for d in friends:
        pl.semaphore_signal(barrier, inc=1, device_id=d, device_id_type=MESH)
    pl.semaphore_wait(barrier, len(friends))

    def remote(src, dst, send, recv, device):
        return pltpu.make_async_remote_copy(
            src_ref=src, dst_ref=dst, send_sem=send, recv_sem=recv, device_id=device, device_id_type=MESH
        )

    def x_copy(d, slot):
        t = others[d]
        return remote(xs.at[d], xg.at[0, slot, j], sem_x.at[0, d], sem_x.at[1, slot], member(t))

    def in_copy(kind, d, slot):
        t = others[d]
        em = energy_of(t, g)
        src = (sp_in, q1_in.at[em], q0_in.at[em], prop_in.at[em])[kind]
        dst = (spg, q1g, q0g, pg)[kind].at[slot]
        return remote(src, dst, sem_in.at[0, kind, d], sem_in.at[1, kind, slot], member(t))

    for d in range(3):
        xs[d] = q1_in[energy_of(others[d], g)].astype(bf16)
        x_copy(d, tme).start()
    for d in range(3):
        in_copy(0, d, tme).start()
    xg[0, tme, j] = q1_in[e].astype(bf16)
    spg[tme] = sp_in[...]
    q1g[tme] = q1_in[e]
    q0g[tme] = q0_in[e]
    pg[tme] = prop_in[e]

    h = 1 - g
    xr, xl, xo = (X + 1) % 4, (X + 3) % 4, (X + 2) % 4
    dev_r, dev_l, dev_p = peer(xr * 2 + g), peer(xl * 2 + g), peer(X * 2 + h)
    dev_rp, dev_lp = peer(xr * 2 + h), peer(xl * 2 + h)

    def ag_ref(it, t, slot, part):
        if part is None:
            return xg.at[it, t, slot]
        return xg.at[it, t, slot, pl.ds(part * HALF, HALF)]

    def ag_send(it, t, k):
        slot, part, dev = (
            (j, None, dev_r),
            (j, None, dev_l),
            (j, None, dev_p),
            (xl * 2 + g, 0, dev_r),
            (xl * 2 + g, 0, dev_rp),
            (xl * 2 + g, None, dev_p),
            (xr * 2 + g, 1, dev_l),
            (xr * 2 + g, 1, dev_lp),
            (xr * 2 + g, None, dev_p),
        )[k]
        ref = ag_ref(it, t, slot, part)
        return remote(ref, ref, sem_ag.at[it, 0, t, k], sem_ag.at[it, 1, t, k], dev)

    def ag_recv(it, t, k):
        slot, part = (
            (xl * 2 + g, None),
            (xr * 2 + g, None),
            (X * 2 + h, None),
            (xo * 2 + g, 0),
            (xo * 2 + h, 0),
            (xl * 2 + h, None),
            (xo * 2 + g, 1),
            (xo * 2 + h, 1),
            (xr * 2 + h, None),
        )[k]
        ref = ag_ref(it, t, slot, part)
        remote(ref, ref, sem_ag.at[it, 0, t, k], sem_ag.at[it, 1, t, k], dev_p).wait_recv()

    def ag_first(it, t):
        for k in (0, 1, 2):
            ag_send(it, t, k).start()

    def ag_second(it, t):
        ag_recv(it, t, 0)
        for k in (4, 3, 5):
            ag_send(it, t, k).start()
        ag_recv(it, t, 1)
        for k in (7, 6, 8):
            ag_send(it, t, k).start()

    def ag_last(it, t):
        for k in range(2, 9):
            ag_recv(it, t, k)

    row_ids = lax.broadcasted_iota(jnp.int32, (4 * ROWS, CH), 0)

    def build(tt):
        def one(ts, carry):
            for half in range(2):
                b = ts * 2 + half
                meta = meta_in[tt, b]
                key = lax.shift_right_logical(meta, 10)
                row = meta & 1023
                tile = spg[tt, b]
                parts = []
                for kt in range(6):
                    mask = jnp.where(key == kt, 1.0, 0.0).astype(bf16)
                    parts.append(tile * mask)
                weights = jnp.concatenate(parts, axis=0)
                hot = jnp.where(row_ids == row, 1.0, 0.0).astype(bf16)
                block = lax.dot_general(weights, hot, (((1,), (1,)), ((), ())), preferred_element_type=f32)
                dmat[ts, tt, :, half * 384 : half * 384 + 384] = block.astype(bf16)
            return carry

        lax.fori_loop(0, 4, one, 0)

    def spline_step(it, ts, first, last):
        def one(tt, carry):
            field = xg[it, ts].reshape(8 * ROWS, CH)
            part = jnp.dot(dmat[ts, tt], field, preferred_element_type=f32)
            if not first:
                part = acc[tt] + part
            if last:
                for k in range(3):
                    u2[tt, :, k * CH : (k + 1) * CH] = part[k * ROWS : (k + 1) * ROWS].astype(bf16)
            else:
                acc[tt] = part
            return carry

        lax.fori_loop(0, 4, one, 0)

    def couple(r):
        dest = (z + r) % 8
        rows = pl.ds(pl.multiple_of(dest * CH, CH), CH)
        total = None
        for k in range(3):
            left = u2[:, :, k * CH : (k + 1) * CH].reshape(4 * ROWS, CH)
            part = lax.dot_general(left, cpl[k, rows, :], (((1,), (1,)), ((), ())), preferred_element_type=f32)
            total = part if total is None else total + part
        pbuf[r] = total.reshape(4, ROWS, CH)

    z_dev = ((pa, (z + 1) % 8), (pa, (z + 7) % 8))

    def rs_copy(it, way, step, t):
        if step == 0:
            src = rs_s.at[it, way, 0, t, pl.ds(way * HALF, HALF)]
            dst = rs_r.at[it, way, 0, t, pl.ds(way * HALF, HALF)]
        elif step == 1:
            src = rs_s.at[it, way, 1, t, pl.ds(way * HALF, HALF)]
            dst = rs_r.at[it, way, 1, t, pl.ds(way * HALF, HALF)]
        elif step == 4:
            src = rs_s.at[it, way, 1, t, pl.ds(HALF - way * HALF, HALF)]
            dst = rs_r.at[it, way, 1, t, pl.ds(HALF - way * HALF, HALF)]
        else:
            src = rs_s.at[it, way, step, t]
            dst = rs_r.at[it, way, step, t]
        return remote(src, dst, sem_rs.at[it, 0, way, step, t], sem_rs.at[it, 1, way, step, t], z_dev[way])

    def rs_begin(it):
        couple(4)

        def one(t, carry):
            for way in range(2):
                lo = way * HALF
                rs_s[it, way, 0, t, lo : lo + HALF] = pbuf[4, t, lo : lo + HALF].astype(bf16)
                rs_copy(it, way, 0, t).start()
            return carry

        lax.fori_loop(0, 4, one, 0)
        couple(3)
        couple(5)

        def early(t, carry):
            for way in range(2):
                hi = HALF - way * HALF
                rs_s[it, way, 1, t, hi : hi + HALF] = pbuf[3 + 2 * way, t, hi : hi + HALF].astype(bf16)
                rs_copy(it, way, 4, t).start()
            return carry

        lax.fori_loop(0, 4, early, 0)

    def rs_step(it, step):
        rel = (4 - step, 4 + step)
        if step > 1:
            couple(rel[0])
            couple(rel[1])

        def one(t, carry):
            for way in range(2):
                rs_copy(it, way, step - 1, t).wait_recv()
                if step == 1:
                    lo = way * HALF
                    rs_s[it, way, 1, t, lo : lo + HALF] = (
                        pbuf[rel[way], t, lo : lo + HALF] + rs_r[it, way, 0, t, lo : lo + HALF].astype(f32)
                    ).astype(bf16)
                else:
                    if step == 2:
                        rs_copy(it, way, 4, t).wait_recv()
                    rs_s[it, way, step, t] = (
                        pbuf[rel[way], t] + rs_r[it, way, step - 1, t].astype(f32)
                    ).astype(bf16)
                rs_copy(it, way, step, t).start()
            return carry

        lax.fori_loop(0, 4, one, 0)

    def rs_end(it, t):
        for way in range(2):
            rs_copy(it, way, 3, t).wait_recv()
        return pbuf[0, t] + (rs_r[it, 0, 3, t].astype(f32) + rs_r[it, 1, 3, t].astype(f32))

    def fold(it, row, value):
        line = jnp.sum(value, axis=0, keepdims=True)
        redv[it, row : row + 1, :] += line[:, :128] + line[:, 128:]

    def ra_copy(it, q, slot):
        return remote(redv.at[it], red_a.at[it, slot], sem_ra.at[it, 0, q], sem_ra.at[it, 1, slot], (pa, q))

    def rb_copy(it, p, slot):
        return remote(redt.at[it], red_b.at[it, slot], sem_rb.at[it, 0, p], sem_rb.at[it, 1, slot], peer(p))

    def reduce_first(it):
        red_a[it, z] = redv[it]
        for q in zs:
            ra_copy(it, q, z).start()

    def reduce_second(it):
        for q in zs:
            ra_copy(it, q, q).wait_recv()
        total = red_a[it, 0]
        for i in range(1, 8):
            total = total + red_a[it, i]
        return total

    def reduce_peers(it, total):
        redt[it] = total
        red_b[it, j] = total
        for p in peers:
            rb_copy(it, p, j).start()

    def reduce_last(it):
        for p in peers:
            rb_copy(it, p, p).wait_recv()
        return finish([red_b[it, i] for i in range(8)])

    def rc_copy(q, slot):
        return remote(redt.at[1], red_c.at[slot], sem_rc.at[0, q], sem_rc.at[1, slot], (q, z))

    def finish(tiles):
        total = tiles[0]
        for tile in tiles[1:]:
            total = total + tile
        sums = jnp.sum(total, axis=1, keepdims=True)
        qw, ss, sq, qq = sums[0:1], sums[1:2], sums[2:3], sums[3:4]
        alpha = qw / CELLS
        rest = 1.0 - alpha
        squares = ss + 2.0 * rest * sq + rest * rest * qq
        beta = jnp.sqrt(jnp.maximum(squares, 0.0) / CELLS + EPS)
        return alpha, rest, beta

    redv[...] = jnp.zeros_like(redv)
    ag_first(0, tme)
    for d in range(3):
        x_copy(d, others[d]).wait_recv()
        ag_first(0, others[d])
    build(tme)
    order = [tme] + others
    for t in order:
        ag_second(0, t)
    for kind in (1, 2, 3):
        for d in range(3):
            in_copy(kind, d, tme).start()
    for d in range(3):
        in_copy(0, d, others[d]).wait_recv()
        build(others[d])
    for t in range(4):
        ag_last(0, t)
        spline_step(0, t, t == 0, t == 3)
    rs_begin(0)
    for step in (1, 2, 3):
        rs_step(0, step)
    couple(0)
    for kind in (1, 2, 3):
        for d in range(3):
            in_copy(kind, d, others[d]).wait_recv()
    beta0 = beta_in[e][0:1, 0:1]

    def first_end(t):
        y = rs_end(0, t)
        y1g[t] = y
        q1 = q1g[t]
        pw = jnp.concatenate([pg[t], pg[t]], axis=1) * y
        s = -pw - beta0 * q0g[t]
        sg[t] = s
        xg[1, t, j] = s.astype(bf16)
        ag_first(1, t)
        fold(0, 0, q1 * (q1 - pw))
        fold(0, 1, s * s)
        fold(0, 2, s * q1)
        fold(0, 3, q1 * q1)

    first_end(0)
    first_end(1)
    ag_second(1, 0)
    first_end(2)
    ag_second(1, 1)
    first_end(3)
    reduce_first(0)

    ag_second(1, 2)
    ag_second(1, 3)
    ag_last(1, 0)
    spline_step(1, 0, True, False)
    reduce_peers(0, reduce_second(0))
    for t in range(1, 4):
        ag_last(1, t)
        spline_step(1, t, False, t == 3)
    rs_begin(1)
    rs_step(1, 1)
    alpha1, rest1, beta1 = reduce_last(0)

    def fin_copy(kind, d, slot):
        t = others[d]
        src = (q2g.at[t], s2g.at[t])[kind]
        dst = (fin_q, fin_s)[kind].at[slot]
        return remote(src, dst, sem_fin.at[0, kind, d], sem_fin.at[1, kind, slot], member(t))

    for t in range(4):
        q2g[t] = (sg[t] + rest1 * q1g[t]) / beta1
    fin_q[e] = q2g[tme]
    for d in range(3):
        fin_copy(0, d, e).start()
    rs_step(1, 2)
    rs_step(1, 3)
    couple(0)
    for t in range(4):
        y = (rs_end(1, t) + rest1 * y1g[t]) / beta1
        q2 = q2g[t]
        pw = jnp.concatenate([pg[t], pg[t]], axis=1) * y
        s = -pw - beta1 * q1g[t]
        s2g[t] = s
        fold(1, 0, q2 * (q2 - pw))
        fold(1, 1, s * s)
        fold(1, 2, s * q2)
        fold(1, 3, q2 * q2)
    reduce_first(1)
    fin_s[e] = s2g[tme]
    for d in range(3):
        fin_copy(1, d, e).start()
    total = reduce_second(1)
    wide = lambda v: jnp.broadcast_to(v, (1, 128))
    total = jnp.concatenate([total[0:4], wide(alpha1), wide(beta1), total[6:8]], axis=0)
    redt[1] = total
    red_c[pa] = total
    for q in plane:
        rc_copy(q, pa).start()
    for kind in range(2):
        for d in range(3):
            fin_copy(kind, d, energy_of(others[d], g)).wait_recv()
    for q in plane:
        rc_copy(q, q).wait_recv()
    lanes = lax.broadcasted_iota(jnp.int32, (1, 128), 1)
    lines = [jnp.zeros((1, 128), f32)] * 4
    for q in range(4):
        tiles = [red_c[i] for i in range(32) if owned(i) == q]
        alpha2, rest2, beta2 = finish(tiles)
        out[q] = (fin_s[q] + rest2 * fin_q[q]) / beta2
        found = (tiles[0][4:5], tiles[0][5:6], wide(alpha2), wide(beta2))
        lines = [jnp.where(lanes == q, new, old) for new, old in zip(found, lines)]
    coef[...] = jnp.concatenate(lines, axis=0)[:, :4]

    for d in range(3):
        x_copy(d, tme).wait_send()
        for kind in range(4):
            in_copy(kind, d, tme).wait_send()
        for kind in range(2):
            fin_copy(kind, d, e).wait_send()
    for it in range(2):

        def drain(t, carry):
            for k in range(9):
                ag_send(it, t, k).wait_send()
            for way in range(2):
                for step in range(5):
                    rs_copy(it, way, step, t).wait_send()
            return carry

        lax.fori_loop(0, 4, drain, 0)
        for q in zs:
            ra_copy(it, q, z).wait_send()
    for p in peers:
        rb_copy(0, p, j).wait_send()
    for q in plane:
        rc_copy(q, pa).wait_send()


def reorder(values):
    tail = values.shape[1:]
    values = values.reshape((4, 4, 2) + tail)
    values = jnp.stack([values[:, :, 0], jnp.roll(values[:, :, 1], -1, axis=1)], axis=2)
    values = values.reshape((2, 2, 2, 2, 2) + tail)
    rest = tuple(range(5, 5 + len(tail)))
    return values.transpose((3, 4, 0, 1, 2) + rest).reshape((8, 4) + tail)


def body(
    basis_prev,
    basis_now,
    beta_prev,
    propagator,
    spline,
    coupling,
    edge_offset,
    edge_tile,
    edge_term,
    edge_count,
):
    f32 = jnp.float32
    bf16 = jnp.bfloat16
    by_energy = lambda v: v.reshape(ROWS, 4, CH).transpose(1, 0, 2)
    q1 = by_energy(basis_now)
    q0 = by_energy(basis_prev)
    prop = jnp.broadcast_to(propagator.reshape(ROWS, 4).T[:, :, None], (4, ROWS, 128))
    beta = jnp.broadcast_to(beta_prev[:, None, None], (4, 8, 128))
    tiles = reorder(spline[:, 0])
    tiles = tiles.transpose(0, 3, 1, 2, 4).reshape(8, HALF, CH)

    X, yp, _ = shifted(lax.axis_index("pa"))
    targets = jnp.stack([place(X, 2 * (yp // 2) + t // 2, t % 2) for t in range(4)])
    live = jnp.arange(4, dtype=jnp.int32)[None, None, :] < edge_count[:, :, None]
    packed = jnp.where(live, edge_term * 2 + edge_tile, 6) * 1024 + edge_offset
    packed = reorder(jnp.take(packed, targets, axis=1))
    packed = packed.transpose(2, 0, 1, 3)[..., None]
    shift = (
        jnp.arange(4, dtype=jnp.int32)[:, None, None] * ROWS + jnp.arange(16, dtype=jnp.int32)[None, None, :]
    )
    meta = (packed + shift).reshape(4, 8, 1, CH)

    vmem = pl.BlockSpec(memory_space=pltpu.VMEM)
    dma = pltpu.SemaphoreType.DMA
    out, coef = pl.pallas_call(
        kernel,
        out_shape=(
            jax.ShapeDtypeStruct((4, ROWS, CH), f32),
            jax.ShapeDtypeStruct((4, 4), f32),
        ),
        in_specs=[vmem] * 7,
        out_specs=(vmem, vmem),
        scratch_shapes=[
            pltpu.VMEM((3, ROWS, CH), bf16),
            pltpu.VMEM((4, 8, HALF, CH), bf16),
            pltpu.VMEM((4, 4, 288, 768), bf16),
            pltpu.VMEM((2, 4, 8, ROWS, CH), bf16),
            pltpu.VMEM((4, 288, CH), f32),
            pltpu.VMEM((4, ROWS, 768), bf16),
            pltpu.VMEM((8, 4, ROWS, CH), f32),
            pltpu.VMEM((2, 2, 4, 4, ROWS, CH), bf16),
            pltpu.VMEM((2, 2, 4, 4, ROWS, CH), bf16),
            pltpu.VMEM((4, ROWS, CH), f32),
            pltpu.VMEM((4, ROWS, CH), f32),
            pltpu.VMEM((4, ROWS, 128), f32),
            pltpu.VMEM((4, ROWS, CH), f32),
            pltpu.VMEM((4, ROWS, CH), f32),
            pltpu.VMEM((4, ROWS, CH), f32),
            pltpu.VMEM((4, ROWS, CH), f32),
            pltpu.VMEM((4, ROWS, CH), f32),
            pltpu.VMEM((4, ROWS, CH), f32),
            pltpu.VMEM((2, 8, 128), f32),
            pltpu.VMEM((2, 8, 8, 128), f32),
            pltpu.VMEM((2, 8, 128), f32),
            pltpu.VMEM((2, 8, 8, 128), f32),
            pltpu.VMEM((32, 8, 128), f32),
            dma((2, 4)),
            dma((2, 4, 4)),
            dma((2, 2, 4, 9)),
            dma((2, 2, 2, 5, 4)),
            dma((2, 2, 8)),
            dma((2, 2, 8)),
            dma((2, 32)),
            dma((2, 2, 4)),
        ],
        compiler_params=pltpu.CompilerParams(
            collective_id=0, has_side_effects=True, vmem_limit_bytes=56 * 1024 * 1024
        ),
    )(q1, q0, beta, prop, tiles, meta, coupling)
    basis_next = out.transpose(1, 0, 2).reshape(2, 48, 4, CH)
    return basis_next, coef


def solution(mesh):
    placed = (
        P("pa", None, None, "ch"),
        P("pa", None, None, "ch"),
        P(),
        P("pa", None, None),
        P(None, "pa", None, None, None),
        P(None, None, "ch"),
        P(),
        P(),
        P(),
        P(),
    )
    return jax.shard_map(
        body,
        mesh=mesh,
        in_specs=placed,
        out_specs=(P("pa", None, None, "ch"), P()),
        check_vma=False,
    )
```

```python
import jax
import jax.numpy as jnp
from jax import lax
from jax.experimental import pallas as pl
from jax.experimental.pallas import tpu as pltpu
from jax.sharding import PartitionSpec as P

MESH = pl.DeviceIdType.MESH
EPS = 1e-06
ROWS = 96
HALF = 48
CH = 256
CELLS = 6291456.0


def shifted(position):
    c = position % 2
    y = (position // 2) % 4
    return position // 8, (y - c + 4) % 4, c


def place(x, yp, c):
    return (x * 4 + (yp + c) % 4) * 2 + c


def owned(position):
    _, yp, c = shifted(position)
    return energy_of((yp % 2) * 2 + c, yp // 2)


def energy_of(t, g):
    return (t % 2) * 2 + 1 - (t // 2 + g) % 2


def source(b, spot):
    th, c = b // 4, (b // 2) % 2
    x = (b % 2) * 2 + (spot >> 1)
    return x * 8 + ((2 * (spot & 1) + th + c) & 3) * 2 + c


def split_energies(raw, parts):
    for q in range(4):
        parts[q] = raw[:, :, q, :].reshape(ROWS, CH)


def turn_tiles(raw, tiles):
    for b in range(8):
        rows = [raw[source(b, i) * 64 : source(b, i) * 64 + 64, :] for i in range(4)]
        block = jnp.concatenate(rows, axis=0).astype(jnp.float32)
        tiles[b] = jnp.transpose(block).astype(jnp.bfloat16)


def spread_edges(edges, meta, x, g):
    n = lax.broadcasted_iota(jnp.int32, (8, 32), 0)
    r = lax.broadcasted_iota(jnp.int32, (8, 32), 1)
    target = (x * 4 + ((2 * g + ((n >> 1) & 1) + (n & 1)) & 3)) * 2 + (n & 1)
    pick = jnp.where(r == target, 1.0, 0.0).astype(jnp.bfloat16)
    over = (((1,), (1,)), ((), ()))
    found = [
        lax.dot_general(pick, edges[i].astype(jnp.bfloat16), over, preferred_element_type=jnp.float32)
        for i in range(2)
    ]
    found = jnp.concatenate(found, axis=0).astype(jnp.bfloat16)
    col = lax.broadcasted_iota(jnp.int32, (128, CH), 1)
    row = lax.broadcasted_iota(jnp.int32, (128, CH), 0)
    lane = lax.broadcasted_iota(jnp.int32, (8, CH), 1)
    for b in range(8):
        wanted = source(b, col >> 6) * 4 + ((col >> 4) & 3)
        widen = jnp.where(row == wanted, 1.0, 0.0).astype(jnp.bfloat16)
        both = jnp.dot(found, widen, preferred_element_type=jnp.float32).astype(jnp.int32)
        meta[b] = both[0:8] * 1024 + both[8:16] + (lane >> 6) * ROWS + (lane & 15)


def spread_propagator(raw, square, parts):
    square[...] = jnp.zeros_like(square)
    for p in range(2):
        square[p * 8 : p * 8 + 4, 0:HALF] = raw[p]
    turned = jnp.transpose(square[...])
    for p in range(2):
        for q in range(4):
            line = turned[0:HALF, p * 8 + q : p * 8 + q + 1]
            parts[q, p * HALF : (p + 1) * HALF, :] = jnp.broadcast_to(line, (HALF, 128))


def kernel(
    q1_raw,
    q0_raw,
    beta_in,
    prop_raw,
    sp_raw,
    edges,
    cpl_hbm,
    out,
    coef,
    cpl,
    q1_in,
    q0_in,
    prop_in,
    square,
    sp_in,
    meta_in,
    xs,
    spg,
    dmat,
    xg,
    acc,
    u2,
    pbuf,
    rs_s,
    rs_r,
    q1g,
    q0g,
    pg,
    y1g,
    sg,
    q2g,
    s2g,
    fin_q,
    fin_s,
    redv,
    red_a,
    redt,
    red_b,
    red_c,
    sem_x,
    sem_in,
    sem_ag,
    sem_rs,
    sem_ra,
    sem_rb,
    sem_rc,
    sem_fin,
    sem_cpl,
):
    pa = lax.axis_index("pa")
    z = lax.axis_index("ch")
    X, yp, c = shifted(pa)
    g = yp // 2
    th = yp % 2
    tme = th * 2 + c
    a = 1 - (th + g) % 2
    e = c * 2 + a
    j = X * 2 + g
    f32 = jnp.float32
    bf16 = jnp.bfloat16

    def member(t):
        return (place(X, 2 * g + t // 2, t % 2), z)

    def peer(jj):
        gg = jj % 2
        return (place(jj // 2, 2 * gg + (gg + 1 - a) % 2, c), z)

    others = [(tme + d) % 4 for d in range(1, 4)]
    peers = [(j + d) % 8 for d in range(1, 8)]
    plane = [(pa + d) % 32 for d in range(1, 32)]
    zs = [(z + d) % 8 for d in range(1, 8)]

    barrier = pltpu.get_barrier_semaphore()
    friends = [(q, z) for q in plane] + [(pa, q) for q in zs]
    for d in friends:
        pl.semaphore_signal(barrier, inc=1, device_id=d, device_id_type=MESH)
    coupling_copy = pltpu.make_async_copy(cpl_hbm, cpl, sem_cpl)
    coupling_copy.start()
    split_energies(q1_raw, q1_in)
    pl.semaphore_wait(barrier, len(friends))

    def remote(src, dst, send, recv, device):
        return pltpu.make_async_remote_copy(
            src_ref=src, dst_ref=dst, send_sem=send, recv_sem=recv, device_id=device, device_id_type=MESH
        )

    def x_copy(d, slot):
        t = others[d]
        return remote(xs.at[d], xg.at[0, slot, j], sem_x.at[0, d], sem_x.at[1, slot], member(t))

    def in_copy(kind, d, slot):
        t = others[d]
        em = energy_of(t, g)
        src = (sp_in, q1_in.at[em], q0_in.at[em], prop_in.at[em])[kind]
        dst = (spg, q1g, q0g, pg)[kind].at[slot]
        return remote(src, dst, sem_in.at[0, kind, d], sem_in.at[1, kind, slot], member(t))

    for d in range(3):
        xs[d] = q1_in[energy_of(others[d], g)].astype(bf16)
        x_copy(d, tme).start()
    xg[0, tme, j] = q1_in[e].astype(bf16)
    turn_tiles(sp_raw, sp_in)
    for d in range(3):
        in_copy(0, d, tme).start()
    spg[tme] = sp_in[...]

    h = 1 - g
    xr, xl, xo = (X + 1) % 4, (X + 3) % 4, (X + 2) % 4
    dev_r, dev_l, dev_p = peer(xr * 2 + g), peer(xl * 2 + g), peer(X * 2 + h)
    dev_rp, dev_lp = peer(xr * 2 + h), peer(xl * 2 + h)

    def ag_ref(it, t, slot, part):
        if part is None:
            return xg.at[it, t, slot]
        return xg.at[it, t, slot, pl.ds(part * HALF, HALF)]

    def ag_send(it, t, k):
        slot, part, dev = (
            (j, None, dev_r),
            (j, None, dev_l),
            (j, None, dev_p),
            (xl * 2 + g, 0, dev_r),
            (xl * 2 + g, 0, dev_rp),
            (xl * 2 + g, None, dev_p),
            (xr * 2 + g, 1, dev_l),
            (xr * 2 + g, 1, dev_lp),
            (xr * 2 + g, None, dev_p),
        )[k]
        ref = ag_ref(it, t, slot, part)
        return remote(ref, ref, sem_ag.at[it, 0, t, k], sem_ag.at[it, 1, t, k], dev)

    def ag_recv(it, t, k):
        slot, part = (
            (xl * 2 + g, None),
            (xr * 2 + g, None),
            (X * 2 + h, None),
            (xo * 2 + g, 0),
            (xo * 2 + h, 0),
            (xl * 2 + h, None),
            (xo * 2 + g, 1),
            (xo * 2 + h, 1),
            (xr * 2 + h, None),
        )[k]
        ref = ag_ref(it, t, slot, part)
        remote(ref, ref, sem_ag.at[it, 0, t, k], sem_ag.at[it, 1, t, k], dev_p).wait_recv()

    def ag_first(it, t):
        for k in (0, 1, 2):
            ag_send(it, t, k).start()

    def ag_second(it, t):
        ag_recv(it, t, 0)
        for k in (4, 3, 5):
            ag_send(it, t, k).start()
        ag_recv(it, t, 1)
        for k in (7, 6, 8):
            ag_send(it, t, k).start()

    def ag_last(it, t):
        for k in range(2, 9):
            ag_recv(it, t, k)

    row_ids = lax.broadcasted_iota(jnp.int32, (4 * ROWS, CH), 0)

    def build(tt):
        def one(ts, carry):
            for half in range(2):
                b = ts * 2 + half
                meta = meta_in[b, pl.ds(tt, 1), :]
                key = lax.shift_right_logical(meta, 10)
                row = meta & 1023
                tile = spg[tt, b]
                parts = []
                for kt in range(6):
                    mask = jnp.where(key == kt, 1.0, 0.0).astype(bf16)
                    parts.append(tile * mask)
                weights = jnp.concatenate(parts, axis=0)
                hot = jnp.where(row_ids == row, 1.0, 0.0).astype(bf16)
                block = lax.dot_general(weights, hot, (((1,), (1,)), ((), ())), preferred_element_type=f32)
                dmat[ts, tt, :, half * 384 : half * 384 + 384] = block.astype(bf16)
            return carry

        lax.fori_loop(0, 4, one, 0)

    def spline_step(it, ts, first, last):
        def one(tt, carry):
            field = xg[it, ts].reshape(8 * ROWS, CH)
            part = jnp.dot(dmat[ts, tt], field, preferred_element_type=f32)
            if not first:
                part = acc[tt] + part
            if last:
                for k in range(3):
                    u2[tt, :, k * CH : (k + 1) * CH] = part[k * ROWS : (k + 1) * ROWS].astype(bf16)
            else:
                acc[tt] = part
            return carry

        lax.fori_loop(0, 4, one, 0)

    def couple(r):
        dest = (z + r) % 8
        rows = pl.ds(pl.multiple_of(dest * CH, CH), CH)
        total = None
        for k in range(3):
            left = u2[:, :, k * CH : (k + 1) * CH].reshape(4 * ROWS, CH)
            part = lax.dot_general(left, cpl[k, rows, :], (((1,), (1,)), ((), ())), preferred_element_type=f32)
            total = part if total is None else total + part
        pbuf[r] = total.reshape(4, ROWS, CH)

    z_dev = ((pa, (z + 1) % 8), (pa, (z + 7) % 8))

    def rs_copy(it, way, step, t):
        if step == 0:
            src = rs_s.at[it, way, 0, t, pl.ds(way * HALF, HALF)]
            dst = rs_r.at[it, way, 0, t, pl.ds(way * HALF, HALF)]
        elif step == 1:
            src = rs_s.at[it, way, 1, t, pl.ds(way * HALF, HALF)]
            dst = rs_r.at[it, way, 1, t, pl.ds(way * HALF, HALF)]
        elif step == 4:
            src = rs_s.at[it, way, 1, t, pl.ds(HALF - way * HALF, HALF)]
            dst = rs_r.at[it, way, 1, t, pl.ds(HALF - way * HALF, HALF)]
        else:
            src = rs_s.at[it, way, step, t]
            dst = rs_r.at[it, way, step, t]
        return remote(src, dst, sem_rs.at[it, 0, way, step, t], sem_rs.at[it, 1, way, step, t], z_dev[way])

    def rs_begin(it):
        couple(4)

        def one(t, carry):
            for way in range(2):
                lo = way * HALF
                rs_s[it, way, 0, t, lo : lo + HALF] = pbuf[4, t, lo : lo + HALF].astype(bf16)
                rs_copy(it, way, 0, t).start()
            return carry

        lax.fori_loop(0, 4, one, 0)
        couple(3)
        couple(5)

        def early(t, carry):
            for way in range(2):
                hi = HALF - way * HALF
                rs_s[it, way, 1, t, hi : hi + HALF] = pbuf[3 + 2 * way, t, hi : hi + HALF].astype(bf16)
                rs_copy(it, way, 4, t).start()
            return carry

        lax.fori_loop(0, 4, early, 0)

    def rs_step(it, step):
        rel = (4 - step, 4 + step)
        if step > 1:
            couple(rel[0])
            couple(rel[1])

        def one(t, carry):
            for way in range(2):
                rs_copy(it, way, step - 1, t).wait_recv()
                if step == 1:
                    lo = way * HALF
                    rs_s[it, way, 1, t, lo : lo + HALF] = (
                        pbuf[rel[way], t, lo : lo + HALF] + rs_r[it, way, 0, t, lo : lo + HALF].astype(f32)
                    ).astype(bf16)
                else:
                    if step == 2:
                        rs_copy(it, way, 4, t).wait_recv()
                    rs_s[it, way, step, t] = (
                        pbuf[rel[way], t] + rs_r[it, way, step - 1, t].astype(f32)
                    ).astype(bf16)
                rs_copy(it, way, step, t).start()
            return carry

        lax.fori_loop(0, 4, one, 0)

    def rs_end(it, t):
        for way in range(2):
            rs_copy(it, way, 3, t).wait_recv()
        return pbuf[0, t] + (rs_r[it, 0, 3, t].astype(f32) + rs_r[it, 1, 3, t].astype(f32))

    def fold(it, row, value):
        line = jnp.sum(value, axis=0, keepdims=True)
        redv[it, row : row + 1, :] += line[:, :128] + line[:, 128:]

    def ra_copy(it, q, slot):
        return remote(redv.at[it], red_a.at[it, slot], sem_ra.at[it, 0, q], sem_ra.at[it, 1, slot], (pa, q))

    def rb_copy(it, p, slot):
        return remote(redt.at[it], red_b.at[it, slot], sem_rb.at[it, 0, p], sem_rb.at[it, 1, slot], peer(p))

    def reduce_first(it):
        red_a[it, z] = redv[it]
        for q in zs:
            ra_copy(it, q, z).start()

    def reduce_second(it):
        for q in zs:
            ra_copy(it, q, q).wait_recv()
        total = red_a[it, 0]
        for i in range(1, 8):
            total = total + red_a[it, i]
        return total

    def reduce_peers(it, total):
        redt[it] = total
        red_b[it, j] = total
        for p in peers:
            rb_copy(it, p, j).start()

    def reduce_last(it):
        for p in peers:
            rb_copy(it, p, p).wait_recv()
        return finish([red_b[it, i] for i in range(8)])

    def rc_copy(q, slot):
        return remote(redt.at[1], red_c.at[slot], sem_rc.at[0, q], sem_rc.at[1, slot], (q, z))

    def finish(tiles):
        total = tiles[0]
        for tile in tiles[1:]:
            total = total + tile
        sums = jnp.sum(total, axis=1, keepdims=True)
        qw, ss, sq, qq = sums[0:1], sums[1:2], sums[2:3], sums[3:4]
        alpha = qw / CELLS
        rest = 1.0 - alpha
        squares = ss + 2.0 * rest * sq + rest * rest * qq
        beta = jnp.sqrt(jnp.maximum(squares, 0.0) / CELLS + EPS)
        return alpha, rest, beta

    redv[...] = jnp.zeros_like(redv)
    ag_first(0, tme)
    for d in range(3):
        x_copy(d, others[d]).wait_recv()
        ag_first(0, others[d])
    spread_edges(edges, meta_in, X, g)
    build(tme)
    order = [tme] + others
    for t in order:
        ag_second(0, t)
    split_energies(q0_raw, q0_in)
    spread_propagator(prop_raw, square, prop_in)
    q1g[tme] = q1_in[e]
    q0g[tme] = q0_in[e]
    pg[tme] = prop_in[e]
    for kind in (1, 2, 3):
        for d in range(3):
            in_copy(kind, d, tme).start()
    for d in range(3):
        in_copy(0, d, others[d]).wait_recv()
        build(others[d])
    for t in range(4):
        ag_last(0, t)
        spline_step(0, t, t == 0, t == 3)
    coupling_copy.wait()
    rs_begin(0)
    for step in (1, 2, 3):
        rs_step(0, step)
    couple(0)
    for kind in (1, 2, 3):
        for d in range(3):
            in_copy(kind, d, others[d]).wait_recv()
    beta0 = beta_in[e]

    def first_end(t):
        y = rs_end(0, t)
        y1g[t] = y
        q1 = q1g[t]
        pw = jnp.concatenate([pg[t], pg[t]], axis=1) * y
        s = -pw - beta0 * q0g[t]
        sg[t] = s
        xg[1, t, j] = s.astype(bf16)
        ag_first(1, t)
        fold(0, 0, q1 * (q1 - pw))
        fold(0, 1, s * s)
        fold(0, 2, s * q1)
        fold(0, 3, q1 * q1)

    first_end(0)
    first_end(1)
    ag_second(1, 0)
    first_end(2)
    ag_second(1, 1)
    first_end(3)
    reduce_first(0)

    ag_second(1, 2)
    ag_second(1, 3)
    ag_last(1, 0)
    spline_step(1, 0, True, False)
    reduce_peers(0, reduce_second(0))
    for t in range(1, 4):
        ag_last(1, t)
        spline_step(1, t, False, t == 3)
    rs_begin(1)
    rs_step(1, 1)
    alpha1, rest1, beta1 = reduce_last(0)

    def fin_copy(kind, d, slot):
        t = others[d]
        src = (q2g.at[t], s2g.at[t])[kind]
        dst = (fin_q, fin_s)[kind].at[slot]
        return remote(src, dst, sem_fin.at[0, kind, d], sem_fin.at[1, kind, slot], member(t))

    for t in range(4):
        q2g[t] = (sg[t] + rest1 * q1g[t]) / beta1
    fin_q[e] = q2g[tme]
    for d in range(3):
        fin_copy(0, d, e).start()
    rs_step(1, 2)
    rs_step(1, 3)
    couple(0)
    for t in range(4):
        y = (rs_end(1, t) + rest1 * y1g[t]) / beta1
        q2 = q2g[t]
        pw = jnp.concatenate([pg[t], pg[t]], axis=1) * y
        s = -pw - beta1 * q1g[t]
        s2g[t] = s
        fold(1, 0, q2 * (q2 - pw))
        fold(1, 1, s * s)
        fold(1, 2, s * q2)
        fold(1, 3, q2 * q2)
    reduce_first(1)
    fin_s[e] = s2g[tme]
    for d in range(3):
        fin_copy(1, d, e).start()
    total = reduce_second(1)
    wide = lambda v: jnp.broadcast_to(v, (1, 128))
    total = jnp.concatenate([total[0:4], wide(alpha1), wide(beta1), total[6:8]], axis=0)
    redt[1] = total
    red_c[pa] = total
    for q in plane:
        rc_copy(q, pa).start()
    for kind in range(2):
        for d in range(3):
            fin_copy(kind, d, energy_of(others[d], g)).wait_recv()
    for q in plane:
        rc_copy(q, q).wait_recv()
    lanes = lax.broadcasted_iota(jnp.int32, (1, 128), 1)
    lines = [jnp.zeros((1, 128), f32)] * 4
    for q in range(4):
        tiles = [red_c[i] for i in range(32) if owned(i) == q]
        alpha2, rest2, beta2 = finish(tiles)
        out[:, :, q, :] = ((fin_s[q] + rest2 * fin_q[q]) / beta2).reshape(2, HALF, CH)
        found = (tiles[0][4:5], tiles[0][5:6], wide(alpha2), wide(beta2))
        lines = [jnp.where(lanes == q, new, old) for new, old in zip(found, lines)]
    coef[...] = jnp.concatenate(lines, axis=0)[:, :4]

    for d in range(3):
        x_copy(d, tme).wait_send()
        for kind in range(4):
            in_copy(kind, d, tme).wait_send()
        for kind in range(2):
            fin_copy(kind, d, e).wait_send()
    for it in range(2):

        def drain(t, carry):
            for k in range(9):
                ag_send(it, t, k).wait_send()
            for way in range(2):
                for step in range(5):
                    rs_copy(it, way, step, t).wait_send()
            return carry

        lax.fori_loop(0, 4, drain, 0)
        for q in zs:
            ra_copy(it, q, z).wait_send()
    for p in peers:
        rb_copy(0, p, j).wait_send()
    for q in plane:
        rc_copy(q, pa).wait_send()


def body(
    basis_prev,
    basis_now,
    beta_prev,
    propagator,
    spline,
    coupling,
    edge_offset,
    edge_tile,
    edge_term,
    edge_count,
):
    f32 = jnp.float32
    bf16 = jnp.bfloat16
    tiles = spline.transpose(0, 1, 2, 4, 3).reshape(2048, HALF)
    live = jnp.arange(4, dtype=jnp.int32)[None, :, None] < edge_count[:, None, :]
    flat = lambda v: v.transpose(0, 2, 1)
    key = jnp.where(live, flat(edge_term) * 2 + flat(edge_tile), 6)
    edges = jnp.stack([key.reshape(128, 32), flat(edge_offset).reshape(128, 32)]).astype(f32)

    vmem = pl.BlockSpec(memory_space=pltpu.VMEM)
    dma = pltpu.SemaphoreType.DMA
    out, coef = pl.pallas_call(
        kernel,
        out_shape=(
            jax.ShapeDtypeStruct((2, HALF, 4, CH), f32),
            jax.ShapeDtypeStruct((4, 4), f32),
        ),
        in_specs=[
            vmem,
            vmem,
            pl.BlockSpec(memory_space=pltpu.SMEM),
            vmem,
            vmem,
            vmem,
            pl.BlockSpec(memory_space=pl.ANY),
        ],
        out_specs=(vmem, vmem),
        scratch_shapes=[
            pltpu.VMEM((3, 2048, CH), bf16),
            pltpu.VMEM((4, ROWS, CH), f32),
            pltpu.VMEM((4, ROWS, CH), f32),
            pltpu.VMEM((4, ROWS, 128), f32),
            pltpu.VMEM((128, 128), f32),
            pltpu.VMEM((8, HALF, CH), bf16),
            pltpu.VMEM((8, 8, CH), jnp.int32),
            pltpu.VMEM((3, ROWS, CH), bf16),
            pltpu.VMEM((4, 8, HALF, CH), bf16),
            pltpu.VMEM((4, 4, 288, 768), bf16),
            pltpu.VMEM((2, 4, 8, ROWS, CH), bf16),
            pltpu.VMEM((4, 288, CH), f32),
            pltpu.VMEM((4, ROWS, 768), bf16),
            pltpu.VMEM((8, 4, ROWS, CH), f32),
            pltpu.VMEM((2, 2, 4, 4, ROWS, CH), bf16),
            pltpu.VMEM((2, 2, 4, 4, ROWS, CH), bf16),
            pltpu.VMEM((4, ROWS, CH), f32),
            pltpu.VMEM((4, ROWS, CH), f32),
            pltpu.VMEM((4, ROWS, 128), f32),
            pltpu.VMEM((4, ROWS, CH), f32),
            pltpu.VMEM((4, ROWS, CH), f32),
            pltpu.VMEM((4, ROWS, CH), f32),
            pltpu.VMEM((4, ROWS, CH), f32),
            pltpu.VMEM((4, ROWS, CH), f32),
            pltpu.VMEM((4, ROWS, CH), f32),
            pltpu.VMEM((2, 8, 128), f32),
            pltpu.VMEM((2, 8, 8, 128), f32),
            pltpu.VMEM((2, 8, 128), f32),
            pltpu.VMEM((2, 8, 8, 128), f32),
            pltpu.VMEM((32, 8, 128), f32),
            dma((2, 4)),
            dma((2, 4, 4)),
            dma((2, 2, 4, 9)),
            dma((2, 2, 2, 5, 4)),
            dma((2, 2, 8)),
            dma((2, 2, 8)),
            dma((2, 32)),
            dma((2, 2, 4)),
            dma(()),
        ],
        compiler_params=pltpu.CompilerParams(
            collective_id=0, has_side_effects=True, vmem_limit_bytes=56 * 1024 * 1024
        ),
    )(basis_now, basis_prev, beta_prev, propagator.transpose(0, 2, 1), tiles, edges, coupling)
    return out, coef


def solution(mesh):
    placed = (
        P("pa", None, None, "ch"),
        P("pa", None, None, "ch"),
        P(),
        P("pa", None, None),
        P(None, "pa", None, None, None),
        P(None, None, "ch"),
        P(),
        P(),
        P(),
        P(),
    )
    return jax.shard_map(
        body,
        mesh=mesh,
        in_specs=placed,
        out_specs=(P("pa", None, None, "ch"), P()),
        check_vma=False,
    )
```

```python
import jax
import jax.numpy as jnp
from jax import lax
from jax.experimental import pallas as pl
from jax.experimental.pallas import tpu as pltpu
from jax.sharding import PartitionSpec as P

MESH = pl.DeviceIdType.MESH
EPS = 1e-06
ROWS = 96
HALF = 48
CH = 256
CELLS = 6291456.0


def shifted(position):
    c = position % 2
    y = (position // 2) % 4
    return position // 8, (y - c + 4) % 4, c


def place(x, yp, c):
    return (x * 4 + (yp + c) % 4) * 2 + c


def owned(position):
    _, yp, c = shifted(position)
    return energy_of((yp % 2) * 2 + c, yp // 2)


def energy_of(t, g):
    return (t % 2) * 2 + 1 - (t // 2 + g) % 2


def source(b, spot):
    th, c = b // 4, (b // 2) % 2
    x = (b % 2) * 2 + (spot >> 1)
    return x * 8 + ((2 * (spot & 1) + th + c) & 3) * 2 + c


def split_energies(raw, parts):
    for q in range(4):
        parts[q] = raw[:, :, q, :].reshape(ROWS, CH)


def turn_tiles(raw, tiles):
    for b in range(8):
        rows = [raw[source(b, i) * 64 : source(b, i) * 64 + 64, :] for i in range(4)]
        block = jnp.concatenate(rows, axis=0).astype(jnp.float32)
        tiles[b] = jnp.transpose(block).astype(jnp.bfloat16)


def spread_edges(offsets, tiles, terms, counts, meta, x, g):
    n = lax.broadcasted_iota(jnp.int32, (8, 32), 0)
    r = lax.broadcasted_iota(jnp.int32, (8, 32), 1)
    target = (x * 4 + ((2 * g + ((n >> 1) & 1) + (n & 1)) & 3)) * 2 + (n & 1)
    pick = jnp.where(r == target, 1.0, 0.0).astype(jnp.bfloat16)
    over = (((1,), (1,)), ((), ()))
    found = []
    for slot in range(4):
        key = jnp.where(slot < counts[...], terms[:, slot, :] * 2 + tiles[:, slot, :], 6)
        both = jnp.concatenate([key, offsets[:, slot, :]], axis=0).astype(jnp.float32).astype(jnp.bfloat16)
        both = lax.dot_general(pick, both, over, preferred_element_type=jnp.float32)
        found.append(jnp.concatenate([both[:, 0:32], both[:, 32:64]], axis=0))
    found = jnp.concatenate(found, axis=1).astype(jnp.bfloat16)
    col = lax.broadcasted_iota(jnp.int32, (128, CH), 1)
    row = lax.broadcasted_iota(jnp.int32, (128, CH), 0)
    lane = lax.broadcasted_iota(jnp.int32, (8, CH), 1)
    for b in range(8):
        wanted = source(b, col >> 6) + ((col >> 4) & 3) * 32
        widen = jnp.where(row == wanted, 1.0, 0.0).astype(jnp.bfloat16)
        both = jnp.dot(found, widen, preferred_element_type=jnp.float32).astype(jnp.int32)
        meta[b] = both[0:8] * 1024 + both[8:16] + (lane >> 6) * ROWS + (lane & 15)


def spread_propagator(raw, square, parts):
    square[...] = jnp.zeros_like(square)
    for p in range(2):
        square[p * 8 : p * 8 + 4, 0:HALF] = raw[p]
    turned = jnp.transpose(square[...])
    for p in range(2):
        for q in range(4):
            line = turned[0:HALF, p * 8 + q : p * 8 + q + 1]
            parts[q, p * HALF : (p + 1) * HALF, :] = jnp.broadcast_to(line, (HALF, 128))


def kernel(
    q1_raw,
    q0_raw,
    beta_in,
    prop_raw,
    sp_raw,
    offset_raw,
    tile_raw,
    term_raw,
    count_raw,
    cpl_hbm,
    out,
    coef,
    cpl,
    q1_in,
    q0_in,
    prop_in,
    square,
    sp_in,
    meta_in,
    xs,
    spg,
    dmat,
    xg,
    acc,
    u2,
    pbuf,
    rs_s,
    rs_r,
    q1g,
    q0g,
    pg,
    y1g,
    sg,
    q2g,
    s2g,
    fin_q,
    fin_s,
    redv,
    red_a,
    redt,
    red_b,
    red_c,
    sem_x,
    sem_in,
    sem_ag,
    sem_rs,
    sem_ra,
    sem_rb,
    sem_rc,
    sem_fin,
    sem_cpl,
):
    pa = lax.axis_index("pa")
    z = lax.axis_index("ch")
    X, yp, c = shifted(pa)
    g = yp // 2
    th = yp % 2
    tme = th * 2 + c
    a = 1 - (th + g) % 2
    e = c * 2 + a
    j = X * 2 + g
    f32 = jnp.float32
    bf16 = jnp.bfloat16

    def member(t):
        return (place(X, 2 * g + t // 2, t % 2), z)

    def peer(jj):
        gg = jj % 2
        return (place(jj // 2, 2 * gg + (gg + 1 - a) % 2, c), z)

    others = [(tme + d) % 4 for d in range(1, 4)]
    peers = [(j + d) % 8 for d in range(1, 8)]
    plane = [(pa + d) % 32 for d in range(1, 32)]
    zs = [(z + d) % 8 for d in range(1, 8)]

    barrier = pltpu.get_barrier_semaphore()
    friends = [(q, z) for q in plane] + [(pa, q) for q in zs]
    for d in friends:
        pl.semaphore_signal(barrier, inc=1, device_id=d, device_id_type=MESH)
    coupling_copy = pltpu.make_async_copy(cpl_hbm, cpl, sem_cpl)
    coupling_copy.start()
    split_energies(q1_raw, q1_in)
    pl.semaphore_wait(barrier, len(friends))

    def remote(src, dst, send, recv, device):
        return pltpu.make_async_remote_copy(
            src_ref=src, dst_ref=dst, send_sem=send, recv_sem=recv, device_id=device, device_id_type=MESH
        )

    def x_copy(d, slot):
        t = others[d]
        return remote(xs.at[d], xg.at[0, slot, j], sem_x.at[0, d], sem_x.at[1, slot], member(t))

    def in_copy(kind, d, slot):
        t = others[d]
        em = energy_of(t, g)
        src = (sp_in, q1_in.at[em], q0_in.at[em], prop_in.at[em])[kind]
        dst = (spg, q1g, q0g, pg)[kind].at[slot]
        return remote(src, dst, sem_in.at[0, kind, d], sem_in.at[1, kind, slot], member(t))

    for d in range(3):
        xs[d] = q1_in[energy_of(others[d], g)].astype(bf16)
        x_copy(d, tme).start()
    xg[0, tme, j] = q1_in[e].astype(bf16)
    turn_tiles(sp_raw, sp_in)
    for d in range(3):
        in_copy(0, d, tme).start()
    spg[tme] = sp_in[...]

    h = 1 - g
    xr, xl, xo = (X + 1) % 4, (X + 3) % 4, (X + 2) % 4
    dev_r, dev_l, dev_p = peer(xr * 2 + g), peer(xl * 2 + g), peer(X * 2 + h)
    dev_rp, dev_lp = peer(xr * 2 + h), peer(xl * 2 + h)

    def ag_ref(it, t, slot, part):
        if part is None:
            return xg.at[it, t, slot]
        return xg.at[it, t, slot, pl.ds(part * HALF, HALF)]

    def ag_send(it, t, k):
        slot, part, dev = (
            (j, None, dev_r),
            (j, None, dev_l),
            (j, None, dev_p),
            (xl * 2 + g, 0, dev_r),
            (xl * 2 + g, 0, dev_rp),
            ((xl * 2 + g, None, dev_p), (X * 2 + h, None, dev_r))[it == 0],
            (xr * 2 + g, 1, dev_l),
            (xr * 2 + g, 1, dev_lp),
            ((xr * 2 + g, None, dev_p), (X * 2 + h, None, dev_l))[it == 0],
        )[k]
        ref = ag_ref(it, t, slot, part)
        return remote(ref, ref, sem_ag.at[it, 0, t, k], sem_ag.at[it, 1, t, k], dev)

    def ag_recv(it, t, k):
        slot, part = (
            (xl * 2 + g, None),
            (xr * 2 + g, None),
            (X * 2 + h, None),
            (xo * 2 + g, 0),
            (xo * 2 + h, 0),
            (xl * 2 + h, None),
            (xo * 2 + g, 1),
            (xo * 2 + h, 1),
            (xr * 2 + h, None),
        )[k]
        ref = ag_ref(it, t, slot, part)
        remote(ref, ref, sem_ag.at[it, 0, t, k], sem_ag.at[it, 1, t, k], dev_p).wait_recv()

    def ag_first(it, t):
        for k in (0, 1, 2):
            ag_send(it, t, k).start()

    def ag_second(it, t):
        if it == 0:
            steps = ((0, (4, 3)), (1, (7, 6)), (2, (5, 8)))
        else:
            steps = ((0, (4, 3, 5)), (1, (7, 6, 8)))
        for arrived, onward in steps:
            ag_recv(it, t, arrived)
            for k in onward:
                ag_send(it, t, k).start()

    def ag_last(it, t):
        for k in range(3 if it == 0 else 2, 9):
            ag_recv(it, t, k)

    row_ids = lax.broadcasted_iota(jnp.int32, (4 * ROWS, CH), 0)

    def build(tt):
        def one(ts, carry):
            for half in range(2):
                b = ts * 2 + half
                meta = meta_in[b, pl.ds(tt, 1), :]
                key = lax.shift_right_logical(meta, 10)
                row = meta & 1023
                tile = spg[tt, b]
                parts = []
                for kt in range(6):
                    mask = jnp.where(key == kt, 1.0, 0.0).astype(bf16)
                    parts.append(tile * mask)
                weights = jnp.concatenate(parts, axis=0)
                hot = jnp.where(row_ids == row, 1.0, 0.0).astype(bf16)
                block = lax.dot_general(weights, hot, (((1,), (1,)), ((), ())), preferred_element_type=f32)
                dmat[ts, tt, :, half * 384 : half * 384 + 384] = block.astype(bf16)
            return carry

        lax.fori_loop(0, 4, one, 0)

    def spline_step(it, ts, first, last):
        def one(tt, carry):
            field = xg[it, ts].reshape(8 * ROWS, CH)
            part = jnp.dot(dmat[ts, tt], field, preferred_element_type=f32)
            if not first:
                part = acc[tt] + part
            if last:
                for k in range(3):
                    u2[tt, :, k * CH : (k + 1) * CH] = part[k * ROWS : (k + 1) * ROWS].astype(bf16)
            else:
                acc[tt] = part
            return carry

        lax.fori_loop(0, 4, one, 0)

    def couple(r):
        dest = (z + r) % 8
        rows = pl.ds(pl.multiple_of(dest * CH, CH), CH)
        total = None
        for k in range(3):
            left = u2[:, :, k * CH : (k + 1) * CH].reshape(4 * ROWS, CH)
            part = lax.dot_general(left, cpl[k, rows, :], (((1,), (1,)), ((), ())), preferred_element_type=f32)
            total = part if total is None else total + part
        pbuf[r] = total.reshape(4, ROWS, CH)

    z_dev = ((pa, (z + 1) % 8), (pa, (z + 7) % 8))

    def rs_copy(it, way, step, t):
        if step == 0:
            src = rs_s.at[it, way, 0, t, pl.ds(way * HALF, HALF)]
            dst = rs_r.at[it, way, 0, t, pl.ds(way * HALF, HALF)]
        elif step == 1:
            src = rs_s.at[it, way, 1, t, pl.ds(way * HALF, HALF)]
            dst = rs_r.at[it, way, 1, t, pl.ds(way * HALF, HALF)]
        elif step == 4:
            src = rs_s.at[it, way, 1, t, pl.ds(HALF - way * HALF, HALF)]
            dst = rs_r.at[it, way, 1, t, pl.ds(HALF - way * HALF, HALF)]
        else:
            src = rs_s.at[it, way, step, t]
            dst = rs_r.at[it, way, step, t]
        return remote(src, dst, sem_rs.at[it, 0, way, step, t], sem_rs.at[it, 1, way, step, t], z_dev[way])

    def rs_begin(it):
        couple(4)

        def one(t, carry):
            for way in range(2):
                lo = way * HALF
                rs_s[it, way, 0, t, lo : lo + HALF] = pbuf[4, t, lo : lo + HALF].astype(bf16)
                rs_copy(it, way, 0, t).start()
            return carry

        lax.fori_loop(0, 4, one, 0)
        couple(3)
        couple(5)

        def early(t, carry):
            for way in range(2):
                hi = HALF - way * HALF
                rs_s[it, way, 1, t, hi : hi + HALF] = pbuf[3 + 2 * way, t, hi : hi + HALF].astype(bf16)
                rs_copy(it, way, 4, t).start()
            return carry

        lax.fori_loop(0, 4, early, 0)

    def rs_step(it, step):
        rel = (4 - step, 4 + step)
        if step > 1:
            couple(rel[0])
            couple(rel[1])

        def one(t, carry):
            for way in range(2):
                rs_copy(it, way, step - 1, t).wait_recv()
                if step == 1:
                    lo = way * HALF
                    rs_s[it, way, 1, t, lo : lo + HALF] = (
                        pbuf[rel[way], t, lo : lo + HALF] + rs_r[it, way, 0, t, lo : lo + HALF].astype(f32)
                    ).astype(bf16)
                else:
                    if step == 2:
                        rs_copy(it, way, 4, t).wait_recv()
                    rs_s[it, way, step, t] = (
                        pbuf[rel[way], t] + rs_r[it, way, step - 1, t].astype(f32)
                    ).astype(bf16)
                rs_copy(it, way, step, t).start()
            return carry

        lax.fori_loop(0, 4, one, 0)

    def rs_end(it, t):
        for way in range(2):
            rs_copy(it, way, 3, t).wait_recv()
        return pbuf[0, t] + (rs_r[it, 0, 3, t].astype(f32) + rs_r[it, 1, 3, t].astype(f32))

    def fold(it, row, value):
        line = jnp.sum(value, axis=0, keepdims=True)
        redv[it, row : row + 1, :] += line[:, :128] + line[:, 128:]

    def ra_copy(it, q, slot):
        return remote(redv.at[it], red_a.at[it, slot], sem_ra.at[it, 0, q], sem_ra.at[it, 1, slot], (pa, q))

    def rb_copy(it, p, slot):
        return remote(redt.at[it], red_b.at[it, slot], sem_rb.at[it, 0, p], sem_rb.at[it, 1, slot], peer(p))

    def reduce_first(it):
        red_a[it, z] = redv[it]
        for q in zs:
            ra_copy(it, q, z).start()

    def reduce_second(it):
        for q in zs:
            ra_copy(it, q, q).wait_recv()
        total = red_a[it, 0]
        for i in range(1, 8):
            total = total + red_a[it, i]
        return total

    def reduce_peers(it, total):
        redt[it] = total
        red_b[it, j] = total
        for p in peers:
            rb_copy(it, p, j).start()

    def reduce_last(it):
        for p in peers:
            rb_copy(it, p, p).wait_recv()
        return finish([red_b[it, i] for i in range(8)])

    def rc_copy(q, slot):
        return remote(redt.at[1], red_c.at[slot], sem_rc.at[0, q], sem_rc.at[1, slot], (q, z))

    def finish(tiles):
        total = tiles[0]
        for tile in tiles[1:]:
            total = total + tile
        sums = jnp.sum(total, axis=1, keepdims=True)
        qw, ss, sq, qq = sums[0:1], sums[1:2], sums[2:3], sums[3:4]
        alpha = qw / CELLS
        rest = 1.0 - alpha
        squares = ss + 2.0 * rest * sq + rest * rest * qq
        beta = jnp.sqrt(jnp.maximum(squares, 0.0) / CELLS + EPS)
        return alpha, rest, beta

    redv[...] = jnp.zeros_like(redv)
    ag_first(0, tme)
    for d in range(3):
        x_copy(d, others[d]).wait_recv()
        ag_first(0, others[d])
    spread_edges(offset_raw, tile_raw, term_raw, count_raw, meta_in, X, g)
    build(tme)
    order = [tme] + others
    for t in order:
        ag_second(0, t)
    split_energies(q0_raw, q0_in)
    spread_propagator(prop_raw, square, prop_in)
    q1g[tme] = q1_in[e]
    q0g[tme] = q0_in[e]
    pg[tme] = prop_in[e]
    for d in range(3):
        in_copy(0, d, others[d]).wait_recv()
        build(others[d])
    for t in range(4):
        ag_last(0, t)
        spline_step(0, t, t == 0, t == 3)
    coupling_copy.wait()
    rs_begin(0)
    for kind in (1, 2, 3):
        for d in range(3):
            in_copy(kind, d, tme).start()
    for step in (1, 2, 3):
        rs_step(0, step)
    couple(0)
    for kind in (1, 2, 3):
        for d in range(3):
            in_copy(kind, d, others[d]).wait_recv()
    beta0 = beta_in[e]

    def first_end(t):
        y = rs_end(0, t)
        y1g[t] = y
        q1 = q1g[t]
        pw = jnp.concatenate([pg[t], pg[t]], axis=1) * y
        s = -pw - beta0 * q0g[t]
        sg[t] = s
        xg[1, t, j] = s.astype(bf16)
        ag_first(1, t)
        fold(0, 0, q1 * (q1 - pw))
        fold(0, 1, s * s)
        fold(0, 2, s * q1)
        fold(0, 3, q1 * q1)

    first_end(0)
    first_end(1)
    ag_second(1, 0)
    first_end(2)
    ag_second(1, 1)
    first_end(3)
    reduce_first(0)

    ag_second(1, 2)
    ag_second(1, 3)
    ag_last(1, 0)
    spline_step(1, 0, True, False)
    reduce_peers(0, reduce_second(0))
    for t in range(1, 4):
        ag_last(1, t)
        spline_step(1, t, False, t == 3)
    rs_begin(1)
    rs_step(1, 1)
    alpha1, rest1, beta1 = reduce_last(0)

    def fin_copy(kind, d, slot):
        t = others[d]
        src = (q2g.at[t], s2g.at[t])[kind]
        dst = (fin_q, fin_s)[kind].at[slot]
        return remote(src, dst, sem_fin.at[0, kind, d], sem_fin.at[1, kind, slot], member(t))

    for t in range(4):
        q2g[t] = (sg[t] + rest1 * q1g[t]) / beta1
    fin_q[e] = q2g[tme]
    for d in range(3):
        fin_copy(0, d, e).start()
    rs_step(1, 2)
    rs_step(1, 3)
    couple(0)
    for t in range(4):
        y = (rs_end(1, t) + rest1 * y1g[t]) / beta1
        q2 = q2g[t]
        pw = jnp.concatenate([pg[t], pg[t]], axis=1) * y
        s = -pw - beta1 * q1g[t]
        s2g[t] = s
        fold(1, 0, q2 * (q2 - pw))
        fold(1, 1, s * s)
        fold(1, 2, s * q2)
        fold(1, 3, q2 * q2)
    reduce_first(1)
    fin_s[e] = s2g[tme]
    for d in range(3):
        fin_copy(1, d, e).start()
    total = reduce_second(1)
    wide = lambda v: jnp.broadcast_to(v, (1, 128))
    total = jnp.concatenate([total[0:4], wide(alpha1), wide(beta1), total[6:8]], axis=0)
    redt[1] = total
    red_c[pa] = total
    for q in plane:
        rc_copy(q, pa).start()
    for kind in range(2):
        for d in range(3):
            fin_copy(kind, d, energy_of(others[d], g)).wait_recv()
    for q in plane:
        rc_copy(q, q).wait_recv()
    lanes = lax.broadcasted_iota(jnp.int32, (1, 128), 1)
    lines = [jnp.zeros((1, 128), f32)] * 4
    for q in range(4):
        tiles = [red_c[i] for i in range(32) if owned(i) == q]
        alpha2, rest2, beta2 = finish(tiles)
        out[:, :, q, :] = ((fin_s[q] + rest2 * fin_q[q]) / beta2).reshape(2, HALF, CH)
        found = (tiles[0][4:5], tiles[0][5:6], wide(alpha2), wide(beta2))
        lines = [jnp.where(lanes == q, new, old) for new, old in zip(found, lines)]
    coef[...] = jnp.concatenate(lines, axis=0)[:, :4]

    for d in range(3):
        x_copy(d, tme).wait_send()
        for kind in range(4):
            in_copy(kind, d, tme).wait_send()
        for kind in range(2):
            fin_copy(kind, d, e).wait_send()
    for it in range(2):

        def drain(t, carry):
            for k in range(9):
                ag_send(it, t, k).wait_send()
            for way in range(2):
                for step in range(5):
                    rs_copy(it, way, step, t).wait_send()
            return carry

        lax.fori_loop(0, 4, drain, 0)
        for q in zs:
            ra_copy(it, q, z).wait_send()
    for p in peers:
        rb_copy(0, p, j).wait_send()
    for q in plane:
        rc_copy(q, pa).wait_send()


def body(
    basis_prev,
    basis_now,
    beta_prev,
    propagator,
    spline,
    coupling,
    edge_offset,
    edge_tile,
    edge_term,
    edge_count,
):
    f32 = jnp.float32
    bf16 = jnp.bfloat16
    tiles = spline.transpose(0, 1, 2, 4, 3).reshape(2048, HALF)
    flat = lambda v: v.transpose(0, 2, 1)

    vmem = pl.BlockSpec(memory_space=pltpu.VMEM)
    dma = pltpu.SemaphoreType.DMA
    out, coef = pl.pallas_call(
        kernel,
        out_shape=(
            jax.ShapeDtypeStruct((2, HALF, 4, CH), f32),
            jax.ShapeDtypeStruct((4, 4), f32),
        ),
        in_specs=[
            vmem,
            vmem,
            pl.BlockSpec(memory_space=pltpu.SMEM),
            vmem,
            vmem,
            vmem,
            vmem,
            vmem,
            vmem,
            pl.BlockSpec(memory_space=pl.ANY),
        ],
        out_specs=(vmem, vmem),
        scratch_shapes=[
            pltpu.VMEM((3, 2048, CH), bf16),
            pltpu.VMEM((4, ROWS, CH), f32),
            pltpu.VMEM((4, ROWS, CH), f32),
            pltpu.VMEM((4, ROWS, 128), f32),
            pltpu.VMEM((128, 128), f32),
            pltpu.VMEM((8, HALF, CH), bf16),
            pltpu.VMEM((8, 8, CH), jnp.int32),
            pltpu.VMEM((3, ROWS, CH), bf16),
            pltpu.VMEM((4, 8, HALF, CH), bf16),
            pltpu.VMEM((4, 4, 288, 768), bf16),
            pltpu.VMEM((2, 4, 8, ROWS, CH), bf16),
            pltpu.VMEM((4, 288, CH), f32),
            pltpu.VMEM((4, ROWS, 768), bf16),
            pltpu.VMEM((8, 4, ROWS, CH), f32),
            pltpu.VMEM((2, 2, 4, 4, ROWS, CH), bf16),
            pltpu.VMEM((2, 2, 4, 4, ROWS, CH), bf16),
            pltpu.VMEM((4, ROWS, CH), f32),
            pltpu.VMEM((4, ROWS, CH), f32),
            pltpu.VMEM((4, ROWS, 128), f32),
            pltpu.VMEM((4, ROWS, CH), f32),
            pltpu.VMEM((4, ROWS, CH), f32),
            pltpu.VMEM((4, ROWS, CH), f32),
            pltpu.VMEM((4, ROWS, CH), f32),
            pltpu.VMEM((4, ROWS, CH), f32),
            pltpu.VMEM((4, ROWS, CH), f32),
            pltpu.VMEM((2, 8, 128), f32),
            pltpu.VMEM((2, 8, 8, 128), f32),
            pltpu.VMEM((2, 8, 128), f32),
            pltpu.VMEM((2, 8, 8, 128), f32),
            pltpu.VMEM((32, 8, 128), f32),
            dma((2, 4)),
            dma((2, 4, 4)),
            dma((2, 2, 4, 9)),
            dma((2, 2, 2, 5, 4)),
            dma((2, 2, 8)),
            dma((2, 2, 8)),
            dma((2, 32)),
            dma((2, 2, 4)),
            dma(()),
        ],
        compiler_params=pltpu.CompilerParams(
            collective_id=0, has_side_effects=True, vmem_limit_bytes=56 * 1024 * 1024
        ),
    )(
        basis_now,
        basis_prev,
        beta_prev,
        flat(propagator),
        tiles,
        flat(edge_offset),
        flat(edge_tile),
        flat(edge_term),
        edge_count,
        coupling,
    )
    return out, coef


def solution(mesh):
    placed = (
        P("pa", None, None, "ch"),
        P("pa", None, None, "ch"),
        P(),
        P("pa", None, None),
        P(None, "pa", None, None, None),
        P(None, None, "ch"),
        P(),
        P(),
        P(),
        P(),
    )
    return jax.shard_map(
        body,
        mesh=mesh,
        in_specs=placed,
        out_specs=(P("pa", None, None, "ch"), P()),
        check_vma=False,
    )
```

```python
import jax
import jax.numpy as jnp
from jax import lax
from jax.experimental import pallas as pl
from jax.experimental.pallas import tpu as pltpu
from jax.sharding import PartitionSpec as P

MESH = pl.DeviceIdType.MESH
EPS = 1e-06
ROWS = 96
HALF = 48
CH = 256
CELLS = 6291456.0


def shifted(position):
    c = position % 2
    y = (position // 2) % 4
    return position // 8, (y - c + 4) % 4, c


def place(x, yp, c):
    return (x * 4 + (yp + c) % 4) * 2 + c


def owned(position):
    _, yp, c = shifted(position)
    return energy_of((yp % 2) * 2 + c, yp // 2)


def energy_of(t, g):
    return (t % 2) * 2 + 1 - (t // 2 + g) % 2


def source(b, spot):
    th, c = b // 4, (b // 2) % 2
    x = (b % 2) * 2 + (spot >> 1)
    return x * 8 + ((2 * (spot & 1) + th + c) & 3) * 2 + c


def split_energies(raw, parts):
    for q in range(4):
        parts[q] = raw[:, :, q, :].reshape(ROWS, CH)


def turn_tiles(raw, tiles):
    for b in range(8):
        rows = [raw[source(b, i) * 64 : source(b, i) * 64 + 64, :] for i in range(4)]
        block = jnp.concatenate(rows, axis=0).astype(jnp.float32)
        tiles[b] = jnp.transpose(block).astype(jnp.bfloat16)


def spread_edges(offsets, tiles, terms, counts, meta, x, g):
    n = lax.broadcasted_iota(jnp.int32, (8, 32), 0)
    r = lax.broadcasted_iota(jnp.int32, (8, 32), 1)
    target = (x * 4 + ((2 * g + ((n >> 1) & 1) + (n & 1)) & 3)) * 2 + (n & 1)
    pick = jnp.where(r == target, 1.0, 0.0).astype(jnp.bfloat16)
    over = (((1,), (1,)), ((), ()))
    found = []
    for slot in range(4):
        key = jnp.where(slot < counts[...], terms[:, slot, :] * 2 + tiles[:, slot, :], 6)
        both = jnp.concatenate([key, offsets[:, slot, :]], axis=0).astype(jnp.float32).astype(jnp.bfloat16)
        both = lax.dot_general(pick, both, over, preferred_element_type=jnp.float32)
        found.append(jnp.concatenate([both[:, 0:32], both[:, 32:64]], axis=0))
    found = jnp.concatenate(found, axis=1).astype(jnp.bfloat16)
    col = lax.broadcasted_iota(jnp.int32, (128, CH), 1)
    row = lax.broadcasted_iota(jnp.int32, (128, CH), 0)
    lane = lax.broadcasted_iota(jnp.int32, (8, CH), 1)
    for b in range(8):
        wanted = source(b, col >> 6) + ((col >> 4) & 3) * 32
        widen = jnp.where(row == wanted, 1.0, 0.0).astype(jnp.bfloat16)
        both = jnp.dot(found, widen, preferred_element_type=jnp.float32).astype(jnp.int32)
        meta[b] = both[0:8] * 1024 + both[8:16] + (lane >> 6) * ROWS + (lane & 15)


def spread_propagator(raw, square, parts):
    square[...] = jnp.zeros_like(square)
    for p in range(2):
        square[p * 8 : p * 8 + 4, 0:HALF] = raw[p]
    turned = jnp.transpose(square[...])
    for p in range(2):
        for q in range(4):
            line = turned[0:HALF, p * 8 + q : p * 8 + q + 1]
            parts[q, p * HALF : (p + 1) * HALF, :] = jnp.broadcast_to(line, (HALF, 128))


def kernel(
    q1_raw_hbm,
    q0_raw_hbm,
    beta_in,
    prop_raw,
    sp_raw_hbm,
    offset_raw_hbm,
    tile_raw_hbm,
    term_raw_hbm,
    count_raw,
    cpl_hbm,
    out,
    coef,
    cpl,
    q1_raw,
    q0_raw,
    sp_raw,
    offset_raw,
    tile_raw,
    term_raw,
    q1_in,
    q0_in,
    prop_in,
    square,
    sp_in,
    meta_in,
    xs,
    spg,
    dmat,
    xg,
    acc,
    u2,
    pbuf,
    rs_s,
    rs_r,
    q1g,
    q0g,
    pg,
    y1g,
    sg,
    q2g,
    s2g,
    fin_q,
    fin_s,
    redv,
    red_a,
    redt,
    red_b,
    red_c,
    sem_x,
    sem_in,
    sem_ag,
    sem_rs,
    sem_ra,
    sem_rb,
    sem_rc,
    sem_fin,
    sem_cpl,
    sem_load,
):
    pa = lax.axis_index("pa")
    z = lax.axis_index("ch")
    X, yp, c = shifted(pa)
    g = yp // 2
    th = yp % 2
    tme = th * 2 + c
    a = 1 - (th + g) % 2
    e = c * 2 + a
    j = X * 2 + g
    f32 = jnp.float32
    bf16 = jnp.bfloat16

    def member(t):
        return (place(X, 2 * g + t // 2, t % 2), z)

    def peer(jj):
        gg = jj % 2
        return (place(jj // 2, 2 * gg + (gg + 1 - a) % 2, c), z)

    others = [(tme + d) % 4 for d in range(1, 4)]
    peers = [(j + d) % 8 for d in range(1, 8)]
    plane = [(pa + d) % 32 for d in range(1, 32)]
    zs = [(z + d) % 8 for d in range(1, 8)]

    barrier = pltpu.get_barrier_semaphore()
    friends = [(q, z) for q in plane] + [(pa, q) for q in zs]
    for d in friends:
        pl.semaphore_signal(barrier, inc=1, device_id=d, device_id_type=MESH)
    coupling_copy = pltpu.make_async_copy(cpl_hbm, cpl, sem_cpl)
    pairs = (
        (q1_raw_hbm, q1_raw),
        (sp_raw_hbm, sp_raw),
        (offset_raw_hbm, offset_raw),
        (tile_raw_hbm, tile_raw),
        (term_raw_hbm, term_raw),
        (q0_raw_hbm, q0_raw),
    )
    loads = [pltpu.make_async_copy(src, dst, sem_load.at[i]) for i, (src, dst) in enumerate(pairs)]
    for load in loads:
        load.start()
    coupling_copy.start()
    loads[0].wait()
    split_energies(q1_raw, q1_in)
    pl.semaphore_wait(barrier, len(friends))

    def remote(src, dst, send, recv, device):
        return pltpu.make_async_remote_copy(
            src_ref=src, dst_ref=dst, send_sem=send, recv_sem=recv, device_id=device, device_id_type=MESH
        )

    def x_copy(d, slot):
        t = others[d]
        return remote(xs.at[d], xg.at[0, slot, j], sem_x.at[0, d], sem_x.at[1, slot], member(t))

    def in_copy(kind, d, slot):
        t = others[d]
        em = energy_of(t, g)
        src = (sp_in, q1_in.at[em], q0_in.at[em], prop_in.at[em])[kind]
        dst = (spg, q1g, q0g, pg)[kind].at[slot]
        return remote(src, dst, sem_in.at[0, kind, d], sem_in.at[1, kind, slot], member(t))

    for d in range(3):
        xs[d] = q1_in[energy_of(others[d], g)].astype(bf16)
        x_copy(d, tme).start()
    xg[0, tme, j] = q1_in[e].astype(bf16)
    loads[1].wait()
    turn_tiles(sp_raw, sp_in)
    for d in range(3):
        in_copy(0, d, tme).start()
    spg[tme] = sp_in[...]

    h = 1 - g
    xr, xl, xo = (X + 1) % 4, (X + 3) % 4, (X + 2) % 4
    dev_r, dev_l, dev_p = peer(xr * 2 + g), peer(xl * 2 + g), peer(X * 2 + h)
    dev_rp, dev_lp = peer(xr * 2 + h), peer(xl * 2 + h)

    def ag_ref(it, t, slot, part):
        if part is None:
            return xg.at[it, t, slot]
        return xg.at[it, t, slot, pl.ds(part * HALF, HALF)]

    def ag_send(it, t, k):
        slot, part, dev = (
            (j, None, dev_r),
            (j, None, dev_l),
            (j, None, dev_p),
            (xl * 2 + g, 0, dev_r),
            (xl * 2 + g, 0, dev_rp),
            ((xl * 2 + g, None, dev_p), (X * 2 + h, None, dev_r))[it == 0],
            (xr * 2 + g, 1, dev_l),
            (xr * 2 + g, 1, dev_lp),
            ((xr * 2 + g, None, dev_p), (X * 2 + h, None, dev_l))[it == 0],
        )[k]
        ref = ag_ref(it, t, slot, part)
        return remote(ref, ref, sem_ag.at[it, 0, t, k], sem_ag.at[it, 1, t, k], dev)

    def ag_recv(it, t, k):
        slot, part = (
            (xl * 2 + g, None),
            (xr * 2 + g, None),
            (X * 2 + h, None),
            (xo * 2 + g, 0),
            (xo * 2 + h, 0),
            (xl * 2 + h, None),
            (xo * 2 + g, 1),
            (xo * 2 + h, 1),
            (xr * 2 + h, None),
        )[k]
        ref = ag_ref(it, t, slot, part)
        remote(ref, ref, sem_ag.at[it, 0, t, k], sem_ag.at[it, 1, t, k], dev_p).wait_recv()

    def ag_first(it, t):
        for k in (0, 1, 2):
            ag_send(it, t, k).start()

    def ag_second(it, t):
        if it == 0:
            steps = ((0, (4, 3)), (1, (7, 6)), (2, (5, 8)))
        else:
            steps = ((0, (4, 3, 5)), (1, (7, 6, 8)))
        for arrived, onward in steps:
            ag_recv(it, t, arrived)
            for k in onward:
                ag_send(it, t, k).start()

    def ag_last(it, t):
        for k in range(3 if it == 0 else 2, 9):
            ag_recv(it, t, k)

    row_ids = lax.broadcasted_iota(jnp.int32, (4 * ROWS, CH), 0)

    def build(tt):
        def one(ts, carry):
            for half in range(2):
                b = ts * 2 + half
                meta = meta_in[b, pl.ds(tt, 1), :]
                key = lax.shift_right_logical(meta, 10)
                row = meta & 1023
                tile = spg[tt, b]
                parts = []
                for kt in range(6):
                    mask = jnp.where(key == kt, 1.0, 0.0).astype(bf16)
                    parts.append(tile * mask)
                weights = jnp.concatenate(parts, axis=0)
                hot = jnp.where(row_ids == row, 1.0, 0.0).astype(bf16)
                block = lax.dot_general(weights, hot, (((1,), (1,)), ((), ())), preferred_element_type=f32)
                dmat[ts, tt, :, half * 384 : half * 384 + 384] = block.astype(bf16)
            return carry

        lax.fori_loop(0, 4, one, 0)

    def spline_step(it, ts, first, last):
        def one(tt, carry):
            field = xg[it, ts].reshape(8 * ROWS, CH)
            part = jnp.dot(dmat[ts, tt], field, preferred_element_type=f32)
            if not first:
                part = acc[tt] + part
            if last:
                for k in range(3):
                    u2[tt, :, k * CH : (k + 1) * CH] = part[k * ROWS : (k + 1) * ROWS].astype(bf16)
            else:
                acc[tt] = part
            return carry

        lax.fori_loop(0, 4, one, 0)

    def couple(r):
        dest = (z + r) % 8
        rows = pl.ds(pl.multiple_of(dest * CH, CH), CH)
        total = None
        for k in range(3):
            left = u2[:, :, k * CH : (k + 1) * CH].reshape(4 * ROWS, CH)
            part = lax.dot_general(left, cpl[k, rows, :], (((1,), (1,)), ((), ())), preferred_element_type=f32)
            total = part if total is None else total + part
        pbuf[r] = total.reshape(4, ROWS, CH)

    z_dev = ((pa, (z + 1) % 8), (pa, (z + 7) % 8))

    def rs_copy(it, way, step, t):
        if step == 0:
            src = rs_s.at[it, way, 0, t, pl.ds(way * HALF, HALF)]
            dst = rs_r.at[it, way, 0, t, pl.ds(way * HALF, HALF)]
        elif step == 1:
            src = rs_s.at[it, way, 1, t, pl.ds(way * HALF, HALF)]
            dst = rs_r.at[it, way, 1, t, pl.ds(way * HALF, HALF)]
        elif step == 4:
            src = rs_s.at[it, way, 1, t, pl.ds(HALF - way * HALF, HALF)]
            dst = rs_r.at[it, way, 1, t, pl.ds(HALF - way * HALF, HALF)]
        else:
            src = rs_s.at[it, way, step, t]
            dst = rs_r.at[it, way, step, t]
        return remote(src, dst, sem_rs.at[it, 0, way, step, t], sem_rs.at[it, 1, way, step, t], z_dev[way])

    def rs_begin(it):
        couple(4)

        def one(t, carry):
            for way in range(2):
                lo = way * HALF
                rs_s[it, way, 0, t, lo : lo + HALF] = pbuf[4, t, lo : lo + HALF].astype(bf16)
                rs_copy(it, way, 0, t).start()
            return carry

        lax.fori_loop(0, 4, one, 0)
        couple(3)
        couple(5)

        def early(t, carry):
            for way in range(2):
                hi = HALF - way * HALF
                rs_s[it, way, 1, t, hi : hi + HALF] = pbuf[3 + 2 * way, t, hi : hi + HALF].astype(bf16)
                rs_copy(it, way, 4, t).start()
            return carry

        lax.fori_loop(0, 4, early, 0)
        for r in (2, 6, 1, 7, 0):
            couple(r)

    def rs_step(it, step):
        rel = (4 - step, 4 + step)

        def one(t, carry):
            for way in range(2):
                rs_copy(it, way, step - 1, t).wait_recv()
                if step == 1:
                    lo = way * HALF
                    rs_s[it, way, 1, t, lo : lo + HALF] = (
                        pbuf[rel[way], t, lo : lo + HALF] + rs_r[it, way, 0, t, lo : lo + HALF].astype(f32)
                    ).astype(bf16)
                else:
                    if step == 2:
                        rs_copy(it, way, 4, t).wait_recv()
                    rs_s[it, way, step, t] = (
                        pbuf[rel[way], t] + rs_r[it, way, step - 1, t].astype(f32)
                    ).astype(bf16)
                rs_copy(it, way, step, t).start()
            return carry

        lax.fori_loop(0, 4, one, 0)

    def rs_end(it, t):
        for way in range(2):
            rs_copy(it, way, 3, t).wait_recv()
        return pbuf[0, t] + (rs_r[it, 0, 3, t].astype(f32) + rs_r[it, 1, 3, t].astype(f32))

    def fold(it, row, value):
        line = jnp.sum(value, axis=0, keepdims=True)
        redv[it, row : row + 1, :] += line[:, :128] + line[:, 128:]

    def ra_copy(it, q, slot):
        return remote(redv.at[it], red_a.at[it, slot], sem_ra.at[it, 0, q], sem_ra.at[it, 1, slot], (pa, q))

    def rb_copy(it, p, slot):
        return remote(redt.at[it], red_b.at[it, slot], sem_rb.at[it, 0, p], sem_rb.at[it, 1, slot], peer(p))

    def reduce_first(it):
        red_a[it, z] = redv[it]
        for q in zs:
            ra_copy(it, q, z).start()

    def reduce_second(it):
        for q in zs:
            ra_copy(it, q, q).wait_recv()
        total = red_a[it, 0]
        for i in range(1, 8):
            total = total + red_a[it, i]
        return total

    def reduce_peers(it, total):
        redt[it] = total
        red_b[it, j] = total
        for p in peers:
            rb_copy(it, p, j).start()

    def reduce_last(it):
        for p in peers:
            rb_copy(it, p, p).wait_recv()
        return finish([red_b[it, i] for i in range(8)])

    def rc_copy(q, slot):
        return remote(redt.at[1], red_c.at[slot], sem_rc.at[0, q], sem_rc.at[1, slot], (q, z))

    def finish(tiles):
        total = tiles[0]
        for tile in tiles[1:]:
            total = total + tile
        sums = jnp.sum(total, axis=1, keepdims=True)
        qw, ss, sq, qq = sums[0:1], sums[1:2], sums[2:3], sums[3:4]
        alpha = qw / CELLS
        rest = 1.0 - alpha
        squares = ss + 2.0 * rest * sq + rest * rest * qq
        beta = jnp.sqrt(jnp.maximum(squares, 0.0) / CELLS + EPS)
        return alpha, rest, beta

    redv[...] = jnp.zeros_like(redv)
    ag_first(0, tme)
    for d in range(3):
        x_copy(d, others[d]).wait_recv()
        ag_first(0, others[d])
    for load in loads[2:5]:
        load.wait()
    spread_edges(offset_raw, tile_raw, term_raw, count_raw, meta_in, X, g)
    build(tme)
    order = [tme] + others
    for t in order:
        ag_second(0, t)
    loads[5].wait()
    split_energies(q0_raw, q0_in)
    spread_propagator(prop_raw, square, prop_in)
    q1g[tme] = q1_in[e]
    q0g[tme] = q0_in[e]
    pg[tme] = prop_in[e]
    for d in range(3):
        in_copy(0, d, others[d]).wait_recv()
        build(others[d])
    for t in range(4):
        ag_last(0, t)
        spline_step(0, t, t == 0, t == 3)
    coupling_copy.wait()
    rs_begin(0)
    for kind in (1, 2, 3):
        for d in range(3):
            in_copy(kind, d, tme).start()
    for step in (1, 2, 3):
        rs_step(0, step)
    for kind in (1, 2, 3):
        for d in range(3):
            in_copy(kind, d, others[d]).wait_recv()
    beta0 = beta_in[e]

    def first_end(t):
        y = rs_end(0, t)
        y1g[t] = y
        q1 = q1g[t]
        pw = jnp.concatenate([pg[t], pg[t]], axis=1) * y
        s = -pw - beta0 * q0g[t]
        sg[t] = s
        xg[1, t, j] = s.astype(bf16)
        ag_first(1, t)
        fold(0, 0, q1 * (q1 - pw))
        fold(0, 1, s * s)
        fold(0, 2, s * q1)
        fold(0, 3, q1 * q1)

    first_end(0)
    first_end(1)
    ag_second(1, 0)
    first_end(2)
    ag_second(1, 1)
    first_end(3)
    reduce_first(0)

    ag_second(1, 2)
    ag_second(1, 3)
    ag_last(1, 0)
    spline_step(1, 0, True, False)
    reduce_peers(0, reduce_second(0))
    for t in range(1, 4):
        ag_last(1, t)
        spline_step(1, t, False, t == 3)
    rs_begin(1)
    rs_step(1, 1)
    alpha1, rest1, beta1 = reduce_last(0)

    def fin_copy(kind, d, slot):
        t = others[d]
        src = (q2g.at[t], s2g.at[t])[kind]
        dst = (fin_q, fin_s)[kind].at[slot]
        return remote(src, dst, sem_fin.at[0, kind, d], sem_fin.at[1, kind, slot], member(t))

    for t in range(4):
        q2g[t] = (sg[t] + rest1 * q1g[t]) / beta1
    fin_q[e] = q2g[tme]
    for d in range(3):
        fin_copy(0, d, e).start()
    rs_step(1, 2)
    rs_step(1, 3)
    for t in range(4):
        y = (rs_end(1, t) + rest1 * y1g[t]) / beta1
        q2 = q2g[t]
        pw = jnp.concatenate([pg[t], pg[t]], axis=1) * y
        s = -pw - beta1 * q1g[t]
        s2g[t] = s
        fold(1, 0, q2 * (q2 - pw))
        fold(1, 1, s * s)
        fold(1, 2, s * q2)
        fold(1, 3, q2 * q2)
    reduce_first(1)
    fin_s[e] = s2g[tme]
    for d in range(3):
        fin_copy(1, d, e).start()
    total = reduce_second(1)
    wide = lambda v: jnp.broadcast_to(v, (1, 128))
    total = jnp.concatenate([total[0:4], wide(alpha1), wide(beta1), total[6:8]], axis=0)
    redt[1] = total
    red_c[pa] = total
    for q in plane:
        rc_copy(q, pa).start()
    for kind in range(2):
        for d in range(3):
            fin_copy(kind, d, energy_of(others[d], g)).wait_recv()
    for q in plane:
        rc_copy(q, q).wait_recv()
    lanes = lax.broadcasted_iota(jnp.int32, (1, 128), 1)
    lines = [jnp.zeros((1, 128), f32)] * 4
    for q in range(4):
        tiles = [red_c[i] for i in range(32) if owned(i) == q]
        alpha2, rest2, beta2 = finish(tiles)
        out[:, :, q, :] = ((fin_s[q] + rest2 * fin_q[q]) / beta2).reshape(2, HALF, CH)
        found = (tiles[0][4:5], tiles[0][5:6], wide(alpha2), wide(beta2))
        lines = [jnp.where(lanes == q, new, old) for new, old in zip(found, lines)]
    coef[...] = jnp.concatenate(lines, axis=0)[:, :4]

    for d in range(3):
        x_copy(d, tme).wait_send()
        for kind in range(4):
            in_copy(kind, d, tme).wait_send()
        for kind in range(2):
            fin_copy(kind, d, e).wait_send()
    for it in range(2):

        def drain(t, carry):
            for k in range(9):
                ag_send(it, t, k).wait_send()
            for way in range(2):
                for step in range(5):
                    rs_copy(it, way, step, t).wait_send()
            return carry

        lax.fori_loop(0, 4, drain, 0)
        for q in zs:
            ra_copy(it, q, z).wait_send()
    for p in peers:
        rb_copy(0, p, j).wait_send()
    for q in plane:
        rc_copy(q, pa).wait_send()


def hand_over(out_in, coef_in, out, coef):
    out[...] = out_in[...]
    coef[...] = coef_in[...]


def body(
    basis_prev,
    basis_now,
    beta_prev,
    propagator,
    spline,
    coupling,
    edge_offset,
    edge_tile,
    edge_term,
    edge_count,
):
    f32 = jnp.float32
    bf16 = jnp.bfloat16
    tiles = spline.transpose(0, 1, 2, 4, 3).reshape(2048, HALF)
    flat = lambda v: v.transpose(0, 2, 1)

    vmem = pl.BlockSpec(memory_space=pltpu.VMEM)
    anywhere = pl.BlockSpec(memory_space=pl.ANY)
    dma = pltpu.SemaphoreType.DMA
    out, coef = pl.pallas_call(
        kernel,
        out_shape=(
            jax.ShapeDtypeStruct((2, HALF, 4, CH), f32),
            jax.ShapeDtypeStruct((4, 4), f32),
        ),
        in_specs=[
            anywhere,
            anywhere,
            pl.BlockSpec(memory_space=pltpu.SMEM),
            vmem,
            anywhere,
            anywhere,
            anywhere,
            anywhere,
            vmem,
            anywhere,
        ],
        out_specs=(vmem, vmem),
        scratch_shapes=[
            pltpu.VMEM((3, 2048, CH), bf16),
            pltpu.VMEM((2, HALF, 4, CH), f32),
            pltpu.VMEM((2, HALF, 4, CH), f32),
            pltpu.VMEM((2048, HALF), bf16),
            pltpu.VMEM((32, 4, 32), jnp.int32),
            pltpu.VMEM((32, 4, 32), jnp.int32),
            pltpu.VMEM((32, 4, 32), jnp.int32),
            pltpu.VMEM((4, ROWS, CH), f32),
            pltpu.VMEM((4, ROWS, CH), f32),
            pltpu.VMEM((4, ROWS, 128), f32),
            pltpu.VMEM((128, 128), f32),
            pltpu.VMEM((8, HALF, CH), bf16),
            pltpu.VMEM((8, 8, CH), jnp.int32),
            pltpu.VMEM((3, ROWS, CH), bf16),
            pltpu.VMEM((4, 8, HALF, CH), bf16),
            pltpu.VMEM((4, 4, 288, 768), bf16),
            pltpu.VMEM((2, 4, 8, ROWS, CH), bf16),
            pltpu.VMEM((4, 288, CH), f32),
            pltpu.VMEM((4, ROWS, 768), bf16),
            pltpu.VMEM((8, 4, ROWS, CH), f32),
            pltpu.VMEM((2, 2, 4, 4, ROWS, CH), bf16),
            pltpu.VMEM((2, 2, 4, 4, ROWS, CH), bf16),
            pltpu.VMEM((4, ROWS, CH), f32),
            pltpu.VMEM((4, ROWS, CH), f32),
            pltpu.VMEM((4, ROWS, 128), f32),
            pltpu.VMEM((4, ROWS, CH), f32),
            pltpu.VMEM((4, ROWS, CH), f32),
            pltpu.VMEM((4, ROWS, CH), f32),
            pltpu.VMEM((4, ROWS, CH), f32),
            pltpu.VMEM((4, ROWS, CH), f32),
            pltpu.VMEM((4, ROWS, CH), f32),
            pltpu.VMEM((2, 8, 128), f32),
            pltpu.VMEM((2, 8, 8, 128), f32),
            pltpu.VMEM((2, 8, 128), f32),
            pltpu.VMEM((2, 8, 8, 128), f32),
            pltpu.VMEM((32, 8, 128), f32),
            dma((2, 4)),
            dma((2, 4, 4)),
            dma((2, 2, 4, 9)),
            dma((2, 2, 2, 5, 4)),
            dma((2, 2, 8)),
            dma((2, 2, 8)),
            dma((2, 32)),
            dma((2, 2, 4)),
            dma(()),
            dma((6,)),
        ],
        compiler_params=pltpu.CompilerParams(
            collective_id=0, has_side_effects=True, vmem_limit_bytes=56 * 1024 * 1024
        ),
    )(
        basis_now,
        basis_prev,
        beta_prev,
        flat(propagator),
        tiles,
        flat(edge_offset),
        flat(edge_tile),
        flat(edge_term),
        edge_count,
        coupling,
    )
    shapes = (jax.ShapeDtypeStruct((2, HALF, 4, CH), f32), jax.ShapeDtypeStruct((4, 4), f32))
    return pl.pallas_call(
        hand_over,
        out_shape=shapes,
        in_specs=[vmem] * 2,
        out_specs=(vmem, vmem),
    )(out, coef)


def solution(mesh):
    placed = (
        P("pa", None, None, "ch"),
        P("pa", None, None, "ch"),
        P(),
        P("pa", None, None),
        P(None, "pa", None, None, None),
        P(None, None, "ch"),
        P(),
        P(),
        P(),
        P(),
    )
    return jax.shard_map(
        body,
        mesh=mesh,
        in_specs=placed,
        out_specs=(P("pa", None, None, "ch"), P()),
        check_vma=False,
    )
```

```python
import jax
import jax.numpy as jnp
from jax import lax
from jax.experimental import pallas as pl
from jax.experimental.pallas import tpu as pltpu
from jax.sharding import PartitionSpec as P

MESH = pl.DeviceIdType.MESH
EPS = 1e-06
ROWS = 96
HALF = 48
CH = 256
CELLS = 6291456.0


def shifted(position):
    c = position % 2
    y = (position // 2) % 4
    return position // 8, (y - c + 4) % 4, c


def place(x, yp, c):
    return (x * 4 + (yp + c) % 4) * 2 + c


def owned(position):
    _, yp, c = shifted(position)
    return energy_of((yp % 2) * 2 + c, yp // 2)


def energy_of(t, g):
    return (t % 2) * 2 + 1 - (t // 2 + g) % 2


def source(b, spot):
    th, c = b // 4, (b // 2) % 2
    x = (b % 2) * 2 + (spot >> 1)
    return x * 8 + ((2 * (spot & 1) + th + c) & 3) * 2 + c


def split_energies(raw, parts):
    for q in range(4):
        parts[q] = raw[:, :, q, :].reshape(ROWS, CH)


def turn_tiles(raw, tiles):
    for b in range(8):
        rows = [raw[source(b, i) * 64 : source(b, i) * 64 + 64, :] for i in range(4)]
        block = jnp.concatenate(rows, axis=0).astype(jnp.float32)
        tiles[b] = jnp.transpose(block).astype(jnp.bfloat16)


def spread_edges(offsets, tiles, terms, counts, meta, x, g):
    n = lax.broadcasted_iota(jnp.int32, (8, 32), 0)
    r = lax.broadcasted_iota(jnp.int32, (8, 32), 1)
    target = (x * 4 + ((2 * g + ((n >> 1) & 1) + (n & 1)) & 3)) * 2 + (n & 1)
    pick = jnp.where(r == target, 1.0, 0.0).astype(jnp.bfloat16)
    over = (((1,), (1,)), ((), ()))
    found = []
    for slot in range(4):
        key = jnp.where(slot < counts[...], terms[:, slot, :] * 2 + tiles[:, slot, :], 6)
        both = jnp.concatenate([key, offsets[:, slot, :]], axis=0).astype(jnp.float32).astype(jnp.bfloat16)
        both = lax.dot_general(pick, both, over, preferred_element_type=jnp.float32)
        found.append(jnp.concatenate([both[:, 0:32], both[:, 32:64]], axis=0))
    found = jnp.concatenate(found, axis=1).astype(jnp.bfloat16)
    col = lax.broadcasted_iota(jnp.int32, (128, CH), 1)
    row = lax.broadcasted_iota(jnp.int32, (128, CH), 0)
    lane = lax.broadcasted_iota(jnp.int32, (8, CH), 1)
    for b in range(8):
        wanted = source(b, col >> 6) + ((col >> 4) & 3) * 32
        widen = jnp.where(row == wanted, 1.0, 0.0).astype(jnp.bfloat16)
        both = jnp.dot(found, widen, preferred_element_type=jnp.float32).astype(jnp.int32)
        meta[b] = both[0:8] * 1024 + both[8:16] + (lane >> 6) * ROWS + (lane & 15)


def spread_propagator(raw, square, parts):
    square[...] = jnp.zeros_like(square)
    for p in range(2):
        square[p * 8 : p * 8 + 4, 0:HALF] = raw[p]
    turned = jnp.transpose(square[...])
    for p in range(2):
        for q in range(4):
            line = turned[0:HALF, p * 8 + q : p * 8 + q + 1]
            parts[q, p * HALF : (p + 1) * HALF, :] = jnp.broadcast_to(line, (HALF, 128))


def kernel(
    q1_raw_hbm,
    q0_raw_hbm,
    beta_in,
    prop_raw,
    sp_raw_hbm,
    offset_raw_hbm,
    tile_raw_hbm,
    term_raw_hbm,
    count_raw,
    cpl_hbm,
    out,
    coef,
    cpl,
    q1_raw,
    q0_raw,
    sp_raw,
    offset_raw,
    tile_raw,
    term_raw,
    q1_in,
    q0_in,
    prop_in,
    square,
    sp_in,
    meta_in,
    xs,
    spg,
    dmat,
    xg,
    acc,
    u2,
    pbuf,
    rs_s,
    rs_r,
    q1g,
    q0g,
    pg,
    y1g,
    sg,
    q2g,
    s2g,
    fin_q,
    fin_s,
    redv,
    red_a,
    redt,
    red_b,
    red_c,
    sem_x,
    sem_in,
    sem_ag,
    sem_rs,
    sem_ra,
    sem_rb,
    sem_rc,
    sem_fin,
    sem_cpl,
    sem_load,
):
    pa = lax.axis_index("pa")
    z = lax.axis_index("ch")
    X, yp, c = shifted(pa)
    g = yp // 2
    th = yp % 2
    tme = th * 2 + c
    a = 1 - (th + g) % 2
    e = c * 2 + a
    j = X * 2 + g
    f32 = jnp.float32
    bf16 = jnp.bfloat16

    def member(t):
        return (place(X, 2 * g + t // 2, t % 2), z)

    def peer(jj):
        gg = jj % 2
        return (place(jj // 2, 2 * gg + (gg + 1 - a) % 2, c), z)

    others = [(tme + d) % 4 for d in range(1, 4)]
    peers = [(j + d) % 8 for d in range(1, 8)]
    plane = [(pa + d) % 32 for d in range(1, 32)]
    zs = [(z + d) % 8 for d in range(1, 8)]

    barrier = pltpu.get_barrier_semaphore()
    friends = [(q, z) for q in plane] + [(pa, q) for q in zs]
    for d in friends:
        pl.semaphore_signal(barrier, inc=1, device_id=d, device_id_type=MESH)
    coupling_copy = pltpu.make_async_copy(cpl_hbm, cpl, sem_cpl)
    pairs = (
        (q1_raw_hbm, q1_raw),
        (sp_raw_hbm, sp_raw),
        (offset_raw_hbm, offset_raw),
        (tile_raw_hbm, tile_raw),
        (term_raw_hbm, term_raw),
        (q0_raw_hbm, q0_raw),
    )
    loads = [pltpu.make_async_copy(src, dst, sem_load.at[i]) for i, (src, dst) in enumerate(pairs)]
    for load in loads:
        load.start()
    coupling_copy.start()
    loads[0].wait()
    split_energies(q1_raw, q1_in)
    pl.semaphore_wait(barrier, len(friends))

    def remote(src, dst, send, recv, device):
        return pltpu.make_async_remote_copy(
            src_ref=src, dst_ref=dst, send_sem=send, recv_sem=recv, device_id=device, device_id_type=MESH
        )

    def x_copy(d, slot):
        t = others[d]
        return remote(xs.at[d], xg.at[0, slot, j], sem_x.at[0, d], sem_x.at[1, slot], member(t))

    def in_copy(kind, d, slot):
        t = others[d]
        em = energy_of(t, g)
        src = (sp_in, q1_in.at[em], q0_in.at[em], prop_in.at[em])[kind]
        dst = (spg, q1g, q0g, pg)[kind].at[slot]
        return remote(src, dst, sem_in.at[0, kind, d], sem_in.at[1, kind, slot], member(t))

    for d in range(3):
        xs[d] = q1_in[energy_of(others[d], g)].astype(bf16)
        x_copy(d, tme).start()
    xg[0, tme, j] = q1_in[e].astype(bf16)
    loads[1].wait()
    turn_tiles(sp_raw, sp_in)
    for d in range(3):
        in_copy(0, d, tme).start()
    spg[tme] = sp_in[...]

    h = 1 - g
    xr, xl, xo = (X + 1) % 4, (X + 3) % 4, (X + 2) % 4
    dev_r, dev_l, dev_p = peer(xr * 2 + g), peer(xl * 2 + g), peer(X * 2 + h)
    dev_rp, dev_lp = peer(xr * 2 + h), peer(xl * 2 + h)

    def ag_ref(it, t, slot, part):
        if part is None:
            return xg.at[it, t, slot]
        return xg.at[it, t, slot, pl.ds(part * HALF, HALF)]

    def ag_send(it, t, k):
        slot, part, dev = (
            (j, None, dev_r),
            (j, None, dev_l),
            (j, None, dev_p),
            (xl * 2 + g, 0, dev_r),
            (xl * 2 + g, 0, dev_rp),
            ((xl * 2 + g, None, dev_p), (X * 2 + h, None, dev_r))[it == 0],
            (xr * 2 + g, 1, dev_l),
            (xr * 2 + g, 1, dev_lp),
            ((xr * 2 + g, None, dev_p), (X * 2 + h, None, dev_l))[it == 0],
        )[k]
        ref = ag_ref(it, t, slot, part)
        return remote(ref, ref, sem_ag.at[it, 0, t, k], sem_ag.at[it, 1, t, k], dev)

    def ag_recv(it, t, k):
        slot, part = (
            (xl * 2 + g, None),
            (xr * 2 + g, None),
            (X * 2 + h, None),
            (xo * 2 + g, 0),
            (xo * 2 + h, 0),
            (xl * 2 + h, None),
            (xo * 2 + g, 1),
            (xo * 2 + h, 1),
            (xr * 2 + h, None),
        )[k]
        ref = ag_ref(it, t, slot, part)
        remote(ref, ref, sem_ag.at[it, 0, t, k], sem_ag.at[it, 1, t, k], dev_p).wait_recv()

    def ag_first(it, t):
        for k in (0, 1, 2):
            ag_send(it, t, k).start()

    def ag_second(it, t):
        if it == 0:
            steps = ((0, (4, 3)), (1, (7, 6)), (2, (5, 8)))
        else:
            steps = ((0, (4, 3, 5)), (1, (7, 6, 8)))
        for arrived, onward in steps:
            ag_recv(it, t, arrived)
            for k in onward:
                ag_send(it, t, k).start()

    def ag_last(it, t):
        for k in range(3 if it == 0 else 2, 9):
            ag_recv(it, t, k)

    row_ids = lax.broadcasted_iota(jnp.int32, (4 * ROWS, CH), 0)

    def build(tt):
        def one(ts, carry):
            for half in range(2):
                b = ts * 2 + half
                meta = meta_in[b, pl.ds(tt, 1), :]
                key = lax.shift_right_logical(meta, 10)
                row = meta & 1023
                tile = spg[tt, b]
                parts = []
                for kt in range(6):
                    mask = jnp.where(key == kt, 1.0, 0.0).astype(bf16)
                    parts.append(tile * mask)
                weights = jnp.concatenate(parts, axis=0)
                hot = jnp.where(row_ids == row, 1.0, 0.0).astype(bf16)
                block = lax.dot_general(weights, hot, (((1,), (1,)), ((), ())), preferred_element_type=f32)
                dmat[ts, tt, :, half * 384 : half * 384 + 384] = block.astype(bf16)
            return carry

        lax.fori_loop(0, 4, one, 0)

    def spline_step(it, ts, first, last):
        def one(tt, carry):
            field = xg[it, ts].reshape(8 * ROWS, CH)
            part = jnp.dot(dmat[ts, tt], field, preferred_element_type=f32)
            if not first:
                part = acc[tt] + part
            if last:
                for k in range(3):
                    u2[tt, :, k * CH : (k + 1) * CH] = part[k * ROWS : (k + 1) * ROWS].astype(bf16)
            else:
                acc[tt] = part
            return carry

        lax.fori_loop(0, 4, one, 0)

    def couple(r):
        dest = (z + r) % 8
        rows = pl.ds(pl.multiple_of(dest * CH, CH), CH)
        total = None
        for k in range(3):
            left = u2[:, :, k * CH : (k + 1) * CH].reshape(4 * ROWS, CH)
            part = lax.dot_general(left, cpl[k, rows, :], (((1,), (1,)), ((), ())), preferred_element_type=f32)
            total = part if total is None else total + part
        pbuf[r] = total.reshape(4, ROWS, CH)

    z_dev = ((pa, (z + 1) % 8), (pa, (z + 7) % 8))

    def rs_copy(it, way, step, t):
        if step == 0:
            src = rs_s.at[it, way, 0, t, pl.ds(way * HALF, HALF)]
            dst = rs_r.at[it, way, 0, t, pl.ds(way * HALF, HALF)]
        elif step == 1:
            src = rs_s.at[it, way, 1, t, pl.ds(way * HALF, HALF)]
            dst = rs_r.at[it, way, 1, t, pl.ds(way * HALF, HALF)]
        elif step == 4:
            src = rs_s.at[it, way, 1, t, pl.ds(HALF - way * HALF, HALF)]
            dst = rs_r.at[it, way, 1, t, pl.ds(HALF - way * HALF, HALF)]
        else:
            src = rs_s.at[it, way, step, t]
            dst = rs_r.at[it, way, step, t]
        return remote(src, dst, sem_rs.at[it, 0, way, step, t], sem_rs.at[it, 1, way, step, t], z_dev[way])

    def rs_begin(it):
        couple(4)

        def one(t, carry):
            for way in range(2):
                lo = way * HALF
                rs_s[it, way, 0, t, lo : lo + HALF] = pbuf[4, t, lo : lo + HALF].astype(bf16)
                rs_copy(it, way, 0, t).start()
            return carry

        lax.fori_loop(0, 4, one, 0)
        couple(3)
        couple(5)

        def early(t, carry):
            for way in range(2):
                hi = HALF - way * HALF
                rs_s[it, way, 1, t, hi : hi + HALF] = pbuf[3 + 2 * way, t, hi : hi + HALF].astype(bf16)
                rs_copy(it, way, 4, t).start()
            return carry

        lax.fori_loop(0, 4, early, 0)
        for r in (2, 6, 1, 7, 0):
            couple(r)

    def rs_step(it, step):
        rel = (4 - step, 4 + step)

        def one(t, carry):
            for way in range(2):
                rs_copy(it, way, step - 1, t).wait_recv()
                if step == 1:
                    lo = way * HALF
                    rs_s[it, way, 1, t, lo : lo + HALF] = (
                        pbuf[rel[way], t, lo : lo + HALF] + rs_r[it, way, 0, t, lo : lo + HALF].astype(f32)
                    ).astype(bf16)
                else:
                    if step == 2:
                        rs_copy(it, way, 4, t).wait_recv()
                    rs_s[it, way, step, t] = (
                        pbuf[rel[way], t] + rs_r[it, way, step - 1, t].astype(f32)
                    ).astype(bf16)
                rs_copy(it, way, step, t).start()
            return carry

        lax.fori_loop(0, 4, one, 0)

    def rs_end(it, t):
        for way in range(2):
            rs_copy(it, way, 3, t).wait_recv()
        return pbuf[0, t] + (rs_r[it, 0, 3, t].astype(f32) + rs_r[it, 1, 3, t].astype(f32))

    def fold(it, row, value):
        line = jnp.sum(value, axis=0, keepdims=True)
        redv[it, row : row + 1, :] += line[:, :128] + line[:, 128:]

    def ra_copy(it, q, slot):
        return remote(redv.at[it], red_a.at[it, slot], sem_ra.at[it, 0, q], sem_ra.at[it, 1, slot], (pa, q))

    def rb_copy(it, p, slot):
        return remote(redt.at[it], red_b.at[it, slot], sem_rb.at[it, 0, p], sem_rb.at[it, 1, slot], peer(p))

    def reduce_first(it):
        red_a[it, z] = redv[it]
        for q in zs:
            ra_copy(it, q, z).start()

    def reduce_second(it):
        for q in zs:
            ra_copy(it, q, q).wait_recv()
        total = red_a[it, 0]
        for i in range(1, 8):
            total = total + red_a[it, i]
        return total

    def reduce_peers(it, total):
        redt[it] = total
        red_b[it, j] = total
        for p in peers:
            rb_copy(it, p, j).start()

    def reduce_last(it):
        for p in peers:
            rb_copy(it, p, p).wait_recv()
        return finish([red_b[it, i] for i in range(8)])

    def rc_copy(q, slot):
        return remote(redt.at[1], red_c.at[slot], sem_rc.at[0, q], sem_rc.at[1, slot], (q, z))

    def finish(tiles):
        total = tiles[0]
        for tile in tiles[1:]:
            total = total + tile
        sums = jnp.sum(total, axis=1, keepdims=True)
        qw, ss, sq, qq = sums[0:1], sums[1:2], sums[2:3], sums[3:4]
        alpha = qw / CELLS
        rest = 1.0 - alpha
        squares = ss + 2.0 * rest * sq + rest * rest * qq
        beta = jnp.sqrt(jnp.maximum(squares, 0.0) / CELLS + EPS)
        return alpha, rest, beta

    redv[...] = jnp.zeros_like(redv)
    ag_first(0, tme)
    for d in range(3):
        x_copy(d, others[d]).wait_recv()
        ag_first(0, others[d])
    for load in loads[2:5]:
        load.wait()
    spread_edges(offset_raw, tile_raw, term_raw, count_raw, meta_in, X, g)
    build(tme)
    order = [tme] + others
    for t in order:
        ag_second(0, t)
    loads[5].wait()
    split_energies(q0_raw, q0_in)
    spread_propagator(prop_raw, square, prop_in)
    q1g[tme] = q1_in[e]
    q0g[tme] = q0_in[e]
    pg[tme] = prop_in[e]
    for d in range(3):
        in_copy(0, d, others[d]).wait_recv()
        build(others[d])
    for t in range(4):
        ag_last(0, t)
        spline_step(0, t, t == 0, t == 3)
    coupling_copy.wait()
    rs_begin(0)
    for kind in (1, 2, 3):
        for d in range(3):
            in_copy(kind, d, tme).start()
    for step in (1, 2, 3):
        rs_step(0, step)
    for kind in (1, 2, 3):
        for d in range(3):
            in_copy(kind, d, others[d]).wait_recv()
    beta0 = beta_in[e]

    def first_end(t):
        y = rs_end(0, t)
        y1g[t] = y
        q1 = q1g[t]
        pw = jnp.concatenate([pg[t], pg[t]], axis=1) * y
        s = -pw - beta0 * q0g[t]
        sg[t] = s
        xg[1, t, j] = s.astype(bf16)
        ag_first(1, t)
        fold(0, 0, q1 * (q1 - pw))
        fold(0, 1, s * s)
        fold(0, 2, s * q1)
        fold(0, 3, q1 * q1)

    for t in range(4):
        first_end(t)
    ag_second(1, 0)
    reduce_first(0)
    ag_second(1, 1)

    ag_second(1, 2)
    ag_second(1, 3)
    ag_last(1, 0)
    spline_step(1, 0, True, False)
    reduce_peers(0, reduce_second(0))
    for t in range(1, 4):
        ag_last(1, t)
        spline_step(1, t, False, t == 3)
    rs_begin(1)
    rs_step(1, 1)
    alpha1, rest1, beta1 = reduce_last(0)

    def fin_copy(kind, d, slot):
        t = others[d]
        src = (q2g.at[t], s2g.at[t])[kind]
        dst = (fin_q, fin_s)[kind].at[slot]
        return remote(src, dst, sem_fin.at[0, kind, d], sem_fin.at[1, kind, slot], member(t))

    for t in range(4):
        q2g[t] = (sg[t] + rest1 * q1g[t]) / beta1
    fin_q[e] = q2g[tme]
    for d in range(3):
        fin_copy(0, d, e).start()
    rs_step(1, 2)
    rs_step(1, 3)
    for t in range(4):
        y = (rs_end(1, t) + rest1 * y1g[t]) / beta1
        q2 = q2g[t]
        pw = jnp.concatenate([pg[t], pg[t]], axis=1) * y
        s = -pw - beta1 * q1g[t]
        s2g[t] = s
        fold(1, 0, q2 * (q2 - pw))
        fold(1, 1, s * s)
        fold(1, 2, s * q2)
        fold(1, 3, q2 * q2)
    reduce_first(1)
    fin_s[e] = s2g[tme]
    for d in range(3):
        fin_copy(1, d, e).start()
    total = reduce_second(1)
    wide = lambda v: jnp.broadcast_to(v, (1, 128))
    total = jnp.concatenate([total[0:4], wide(alpha1), wide(beta1), total[6:8]], axis=0)
    redt[1] = total
    red_c[pa] = total
    for q in plane:
        rc_copy(q, pa).start()
    for kind in range(2):
        for d in range(3):
            fin_copy(kind, d, energy_of(others[d], g)).wait_recv()
        for q in range(4):
            (q1_raw, q0_raw)[kind][:, :, q, :] = (fin_q, fin_s)[kind][q].reshape(2, HALF, CH)
    for q in plane:
        rc_copy(q, q).wait_recv()
    lanes = lax.broadcasted_iota(jnp.int32, (1, 128), 1)
    lines = [jnp.zeros((1, 128), f32)] * 4
    rests, scales = [], []
    for q in range(4):
        tiles = [red_c[i] for i in range(32) if owned(i) == q]
        alpha2, rest2, beta2 = finish(tiles)
        rests.append(rest2)
        scales.append(1.0 / beta2)
        found = (tiles[0][4:5], tiles[0][5:6], wide(alpha2), wide(beta2))
        lines = [jnp.where(lanes == q, new, old) for new, old in zip(found, lines)]
    coef[...] = jnp.concatenate(lines, axis=0)[:, :4]
    column = lambda v: jnp.broadcast_to(jnp.concatenate(v, axis=0), (4, CH))[None, None]
    out[...] = (q0_raw[...] + column(rests) * q1_raw[...]) * column(scales)

    for d in range(3):
        x_copy(d, tme).wait_send()
        for kind in range(4):
            in_copy(kind, d, tme).wait_send()
        for kind in range(2):
            fin_copy(kind, d, e).wait_send()
    for it in range(2):

        def drain(t, carry):
            for k in range(9):
                ag_send(it, t, k).wait_send()
            for way in range(2):
                for step in range(5):
                    rs_copy(it, way, step, t).wait_send()
            return carry

        lax.fori_loop(0, 4, drain, 0)
        for q in zs:
            ra_copy(it, q, z).wait_send()
    for p in peers:
        rb_copy(0, p, j).wait_send()
    for q in plane:
        rc_copy(q, pa).wait_send()


def hand_over(out_in, coef_in, out, coef):
    out[...] = out_in[...]
    coef[...] = coef_in[...]


def body(
    basis_prev,
    basis_now,
    beta_prev,
    propagator,
    spline,
    coupling,
    edge_offset,
    edge_tile,
    edge_term,
    edge_count,
):
    f32 = jnp.float32
    bf16 = jnp.bfloat16
    tiles = spline.transpose(0, 1, 2, 4, 3).reshape(2048, HALF)
    flat = lambda v: v.transpose(0, 2, 1)

    vmem = pl.BlockSpec(memory_space=pltpu.VMEM)
    anywhere = pl.BlockSpec(memory_space=pl.ANY)
    dma = pltpu.SemaphoreType.DMA
    out, coef = pl.pallas_call(
        kernel,
        out_shape=(
            jax.ShapeDtypeStruct((2, HALF, 4, CH), f32),
            jax.ShapeDtypeStruct((4, 4), f32),
        ),
        in_specs=[
            anywhere,
            anywhere,
            pl.BlockSpec(memory_space=pltpu.SMEM),
            vmem,
            anywhere,
            anywhere,
            anywhere,
            anywhere,
            vmem,
            anywhere,
        ],
        out_specs=(vmem, vmem),
        scratch_shapes=[
            pltpu.VMEM((3, 2048, CH), bf16),
            pltpu.VMEM((2, HALF, 4, CH), f32),
            pltpu.VMEM((2, HALF, 4, CH), f32),
            pltpu.VMEM((2048, HALF), bf16),
            pltpu.VMEM((32, 4, 32), jnp.int32),
            pltpu.VMEM((32, 4, 32), jnp.int32),
            pltpu.VMEM((32, 4, 32), jnp.int32),
            pltpu.VMEM((4, ROWS, CH), f32),
            pltpu.VMEM((4, ROWS, CH), f32),
            pltpu.VMEM((4, ROWS, 128), f32),
            pltpu.VMEM((128, 128), f32),
            pltpu.VMEM((8, HALF, CH), bf16),
            pltpu.VMEM((8, 8, CH), jnp.int32),
            pltpu.VMEM((3, ROWS, CH), bf16),
            pltpu.VMEM((4, 8, HALF, CH), bf16),
            pltpu.VMEM((4, 4, 288, 768), bf16),
            pltpu.VMEM((2, 4, 8, ROWS, CH), bf16),
            pltpu.VMEM((4, 288, CH), f32),
            pltpu.VMEM((4, ROWS, 768), bf16),
            pltpu.VMEM((8, 4, ROWS, CH), f32),
            pltpu.VMEM((2, 2, 4, 4, ROWS, CH), bf16),
            pltpu.VMEM((2, 2, 4, 4, ROWS, CH), bf16),
            pltpu.VMEM((4, ROWS, CH), f32),
            pltpu.VMEM((4, ROWS, CH), f32),
            pltpu.VMEM((4, ROWS, 128), f32),
            pltpu.VMEM((4, ROWS, CH), f32),
            pltpu.VMEM((4, ROWS, CH), f32),
            pltpu.VMEM((4, ROWS, CH), f32),
            pltpu.VMEM((4, ROWS, CH), f32),
            pltpu.VMEM((4, ROWS, CH), f32),
            pltpu.VMEM((4, ROWS, CH), f32),
            pltpu.VMEM((2, 8, 128), f32),
            pltpu.VMEM((2, 8, 8, 128), f32),
            pltpu.VMEM((2, 8, 128), f32),
            pltpu.VMEM((2, 8, 8, 128), f32),
            pltpu.VMEM((32, 8, 128), f32),
            dma((2, 4)),
            dma((2, 4, 4)),
            dma((2, 2, 4, 9)),
            dma((2, 2, 2, 5, 4)),
            dma((2, 2, 8)),
            dma((2, 2, 8)),
            dma((2, 32)),
            dma((2, 2, 4)),
            dma(()),
            dma((6,)),
        ],
        compiler_params=pltpu.CompilerParams(
            collective_id=0, has_side_effects=True, vmem_limit_bytes=56 * 1024 * 1024
        ),
    )(
        basis_now,
        basis_prev,
        beta_prev,
        flat(propagator),
        tiles,
        flat(edge_offset),
        flat(edge_tile),
        flat(edge_term),
        edge_count,
        coupling,
    )
    shapes = (jax.ShapeDtypeStruct((2, HALF, 4, CH), f32), jax.ShapeDtypeStruct((4, 4), f32))
    return pl.pallas_call(
        hand_over,
        out_shape=shapes,
        in_specs=[vmem] * 2,
        out_specs=(vmem, vmem),
    )(out, coef)


def solution(mesh):
    placed = (
        P("pa", None, None, "ch"),
        P("pa", None, None, "ch"),
        P(),
        P("pa", None, None),
        P(None, "pa", None, None, None),
        P(None, None, "ch"),
        P(),
        P(),
        P(),
        P(),
    )
    return jax.shard_map(
        body,
        mesh=mesh,
        in_specs=placed,
        out_specs=(P("pa", None, None, "ch"), P()),
        check_vma=False,
    )
```

```python
import jax
import jax.numpy as jnp
from jax import lax
from jax.experimental import pallas as pl
from jax.experimental.pallas import tpu as pltpu
from jax.sharding import PartitionSpec as P

MESH = pl.DeviceIdType.MESH
EPS = 1e-06
ROWS = 96
HALF = 48
CH = 256
CELLS = 6291456.0


def shifted(position):
    c = position % 2
    y = (position // 2) % 4
    return position // 8, (y - c + 4) % 4, c


def place(x, yp, c):
    return (x * 4 + (yp + c) % 4) * 2 + c


def owned(position):
    _, yp, c = shifted(position)
    return energy_of((yp % 2) * 2 + c, yp // 2)


def energy_of(t, g):
    return (t % 2) * 2 + 1 - (t // 2 + g) % 2


def source(b, spot):
    th, c = b // 4, (b // 2) % 2
    x = (b % 2) * 2 + (spot >> 1)
    return x * 8 + ((2 * (spot & 1) + th + c) & 3) * 2 + c


def split_energies(raw, parts):
    for q in range(4):
        parts[q] = raw[:, :, q, :].reshape(ROWS, CH)


def turn_tiles(raw, tiles):
    for b in range(8):
        rows = [raw[source(b, i) * 64 : source(b, i) * 64 + 64, :] for i in range(4)]
        block = jnp.concatenate(rows, axis=0).astype(jnp.float32)
        tiles[b] = jnp.transpose(block).astype(jnp.bfloat16)


def spread_edges(offsets, tiles, terms, counts, meta, x, g):
    n = lax.broadcasted_iota(jnp.int32, (8, 32), 0)
    r = lax.broadcasted_iota(jnp.int32, (8, 32), 1)
    target = (x * 4 + ((2 * g + ((n >> 1) & 1) + (n & 1)) & 3)) * 2 + (n & 1)
    pick = jnp.where(r == target, 1.0, 0.0).astype(jnp.bfloat16)
    over = (((1,), (1,)), ((), ()))
    found = []
    for slot in range(4):
        key = jnp.where(slot < counts[...], terms[:, slot, :] * 2 + tiles[:, slot, :], 6)
        both = jnp.concatenate([key, offsets[:, slot, :]], axis=0).astype(jnp.float32).astype(jnp.bfloat16)
        both = lax.dot_general(pick, both, over, preferred_element_type=jnp.float32)
        found.append(jnp.concatenate([both[:, 0:32], both[:, 32:64]], axis=0))
    found = jnp.concatenate(found, axis=1).astype(jnp.bfloat16)
    col = lax.broadcasted_iota(jnp.int32, (128, CH), 1)
    row = lax.broadcasted_iota(jnp.int32, (128, CH), 0)
    lane = lax.broadcasted_iota(jnp.int32, (8, CH), 1)
    for b in range(8):
        wanted = source(b, col >> 6) + ((col >> 4) & 3) * 32
        widen = jnp.where(row == wanted, 1.0, 0.0).astype(jnp.bfloat16)
        both = jnp.dot(found, widen, preferred_element_type=jnp.float32).astype(jnp.int32)
        meta[b] = both[0:8] * 1024 + both[8:16] + (lane >> 6) * ROWS + (lane & 15)


def spread_propagator(raw, square, parts):
    square[...] = jnp.zeros_like(square)
    for p in range(2):
        square[p * 8 : p * 8 + 4, 0:HALF] = raw[p]
    turned = jnp.transpose(square[...])
    for p in range(2):
        for q in range(4):
            line = turned[0:HALF, p * 8 + q : p * 8 + q + 1]
            parts[q, p * HALF : (p + 1) * HALF, :] = jnp.broadcast_to(line, (HALF, 128))


def kernel(
    q1_raw_hbm,
    q0_raw_hbm,
    beta_in,
    prop_raw,
    sp_raw_hbm,
    offset_raw_hbm,
    tile_raw_hbm,
    term_raw_hbm,
    count_raw,
    cpl_hbm,
    out,
    coef,
    cpl,
    q1_raw,
    q0_raw,
    sp_raw,
    offset_raw,
    tile_raw,
    term_raw,
    q1_in,
    q0_in,
    prop_in,
    square,
    sp_in,
    meta_in,
    xs,
    spg,
    dmat,
    xg,
    acc,
    u2,
    pbuf,
    rs_s,
    rs_r,
    q1g,
    q0g,
    pg,
    y1g,
    sg,
    q2g,
    s2g,
    fin_q,
    fin_s,
    redv,
    red_a,
    redt,
    red_b,
    red_c,
    sem_x,
    sem_in,
    sem_ag,
    sem_rs,
    sem_ra,
    sem_rb,
    sem_rc,
    sem_fin,
    sem_cpl,
    sem_load,
):
    pa = lax.axis_index("pa")
    z = lax.axis_index("ch")
    X, yp, c = shifted(pa)
    g = yp // 2
    th = yp % 2
    tme = th * 2 + c
    a = 1 - (th + g) % 2
    e = c * 2 + a
    j = X * 2 + g
    f32 = jnp.float32
    bf16 = jnp.bfloat16

    def member(t):
        return (place(X, 2 * g + t // 2, t % 2), z)

    def peer(jj):
        gg = jj % 2
        return (place(jj // 2, 2 * gg + (gg + 1 - a) % 2, c), z)

    others = [(tme + d) % 4 for d in range(1, 4)]
    peers = [(j + d) % 8 for d in range(1, 8)]
    plane = [(pa + d) % 32 for d in range(1, 32)]
    zs = [(z + d) % 8 for d in range(1, 8)]

    barrier = pltpu.get_barrier_semaphore()
    friends = [(q, z) for q in plane] + [(pa, q) for q in zs]
    for d in friends:
        pl.semaphore_signal(barrier, inc=1, device_id=d, device_id_type=MESH)
    coupling_copy = pltpu.make_async_copy(cpl_hbm, cpl, sem_cpl)
    pairs = (
        (q1_raw_hbm, q1_raw),
        (sp_raw_hbm, sp_raw),
        (offset_raw_hbm, offset_raw),
        (tile_raw_hbm, tile_raw),
        (term_raw_hbm, term_raw),
        (q0_raw_hbm, q0_raw),
    )
    loads = [pltpu.make_async_copy(src, dst, sem_load.at[i]) for i, (src, dst) in enumerate(pairs)]
    for load in loads:
        load.start()
    coupling_copy.start()
    loads[0].wait()
    split_energies(q1_raw, q1_in)
    pl.semaphore_wait(barrier, len(friends))

    def remote(src, dst, send, recv, device):
        return pltpu.make_async_remote_copy(
            src_ref=src, dst_ref=dst, send_sem=send, recv_sem=recv, device_id=device, device_id_type=MESH
        )

    def x_copy(d, slot):
        t = others[d]
        return remote(xs.at[d], xg.at[0, slot, j], sem_x.at[0, d], sem_x.at[1, slot], member(t))

    def in_copy(kind, d, slot):
        t = others[d]
        em = energy_of(t, g)
        src = (sp_in, q1_in.at[em], q0_in.at[em], prop_in.at[em])[kind]
        dst = (spg, q1g, q0g, pg)[kind].at[slot]
        return remote(src, dst, sem_in.at[0, kind, d], sem_in.at[1, kind, slot], member(t))

    for d in range(3):
        xs[d] = q1_in[energy_of(others[d], g)].astype(bf16)
        x_copy(d, tme).start()
    xg[0, tme, j] = q1_in[e].astype(bf16)
    loads[1].wait()
    turn_tiles(sp_raw, sp_in)
    for d in range(3):
        in_copy(0, d, tme).start()
    spg[tme] = sp_in[...]

    h = 1 - g
    xr, xl, xo = (X + 1) % 4, (X + 3) % 4, (X + 2) % 4
    dev_r, dev_l, dev_p = peer(xr * 2 + g), peer(xl * 2 + g), peer(X * 2 + h)
    dev_rp, dev_lp = peer(xr * 2 + h), peer(xl * 2 + h)

    def ag_ref(it, t, slot, part):
        if part is None:
            return xg.at[it, t, slot]
        return xg.at[it, t, slot, pl.ds(part * HALF, HALF)]

    def ag_send(it, t, k):
        slot, part, dev = (
            (j, None, dev_r),
            (j, None, dev_l),
            (j, None, dev_p),
            (xl * 2 + g, 0, dev_r),
            (xl * 2 + g, 0, dev_rp),
            ((xl * 2 + g, None, dev_p), (X * 2 + h, None, dev_r))[it == 0],
            (xr * 2 + g, 1, dev_l),
            (xr * 2 + g, 1, dev_lp),
            ((xr * 2 + g, None, dev_p), (X * 2 + h, None, dev_l))[it == 0],
        )[k]
        ref = ag_ref(it, t, slot, part)
        return remote(ref, ref, sem_ag.at[it, 0, t, k], sem_ag.at[it, 1, t, k], dev)

    def ag_recv(it, t, k):
        slot, part = (
            (xl * 2 + g, None),
            (xr * 2 + g, None),
            (X * 2 + h, None),
            (xo * 2 + g, 0),
            (xo * 2 + h, 0),
            (xl * 2 + h, None),
            (xo * 2 + g, 1),
            (xo * 2 + h, 1),
            (xr * 2 + h, None),
        )[k]
        ref = ag_ref(it, t, slot, part)
        remote(ref, ref, sem_ag.at[it, 0, t, k], sem_ag.at[it, 1, t, k], dev_p).wait_recv()

    def ag_first(it, t):
        for k in (0, 1, 2):
            ag_send(it, t, k).start()

    def ag_second(it, t):
        if it == 0:
            steps = ((0, (4, 3)), (1, (7, 6)), (2, (5, 8)))
        else:
            steps = ((0, (4, 3, 5)), (1, (7, 6, 8)))
        for arrived, onward in steps:
            ag_recv(it, t, arrived)
            for k in onward:
                ag_send(it, t, k).start()

    def ag_last(it, t):
        for k in range(3 if it == 0 else 2, 9):
            ag_recv(it, t, k)

    row_ids = lax.broadcasted_iota(jnp.int32, (4 * ROWS, CH), 0)

    def build(tt):
        def one(ts, carry):
            for half in range(2):
                b = ts * 2 + half
                meta = meta_in[b, pl.ds(tt, 1), :]
                key = lax.shift_right_logical(meta, 10)
                row = meta & 1023
                tile = spg[tt, b]
                parts = []
                for kt in range(6):
                    mask = jnp.where(key == kt, 1.0, 0.0).astype(bf16)
                    parts.append(tile * mask)
                weights = jnp.concatenate(parts, axis=0)
                hot = jnp.where(row_ids == row, 1.0, 0.0).astype(bf16)
                block = lax.dot_general(weights, hot, (((1,), (1,)), ((), ())), preferred_element_type=f32)
                dmat[ts, tt, :, half * 384 : half * 384 + 384] = block.astype(bf16)
            return carry

        lax.fori_loop(0, 4, one, 0)

    def spline_step(it, ts, first, last):
        def one(tt, carry):
            field = xg[it, ts].reshape(8 * ROWS, CH)
            part = jnp.dot(dmat[ts, tt], field, preferred_element_type=f32)
            if not first:
                part = acc[tt] + part
            if last:
                for k in range(3):
                    u2[tt, :, k * CH : (k + 1) * CH] = part[k * ROWS : (k + 1) * ROWS].astype(bf16)
            else:
                acc[tt] = part
            return carry

        lax.fori_loop(0, 4, one, 0)

    def couple(r):
        dest = (z + r) % 8
        rows = pl.ds(pl.multiple_of(dest * CH, CH), CH)
        total = None
        for k in range(3):
            left = u2[:, :, k * CH : (k + 1) * CH].reshape(4 * ROWS, CH)
            part = lax.dot_general(left, cpl[k, rows, :], (((1,), (1,)), ((), ())), preferred_element_type=f32)
            total = part if total is None else total + part
        pbuf[r] = total.reshape(4, ROWS, CH)

    z_dev = ((pa, (z + 1) % 8), (pa, (z + 7) % 8))

    def rs_copy(it, way, step, t):
        if step == 0:
            src = rs_s.at[it, way, 0, t, pl.ds(way * HALF, HALF)]
            dst = rs_r.at[it, way, 0, t, pl.ds(way * HALF, HALF)]
        elif step == 1:
            src = rs_s.at[it, way, 1, t, pl.ds(way * HALF, HALF)]
            dst = rs_r.at[it, way, 1, t, pl.ds(way * HALF, HALF)]
        elif step == 4:
            src = rs_s.at[it, way, 1, t, pl.ds(HALF - way * HALF, HALF)]
            dst = rs_r.at[it, way, 1, t, pl.ds(HALF - way * HALF, HALF)]
        else:
            src = rs_s.at[it, way, step, t]
            dst = rs_r.at[it, way, step, t]
        return remote(src, dst, sem_rs.at[it, 0, way, step, t], sem_rs.at[it, 1, way, step, t], z_dev[way])

    def rs_begin(it):
        couple(4)

        def one(t, carry):
            for way in range(2):
                lo = way * HALF
                rs_s[it, way, 0, t, lo : lo + HALF] = pbuf[4, t, lo : lo + HALF].astype(bf16)
                rs_copy(it, way, 0, t).start()
            return carry

        lax.fori_loop(0, 4, one, 0)
        couple(3)
        couple(5)

        def early(t, carry):
            for way in range(2):
                hi = HALF - way * HALF
                rs_s[it, way, 1, t, hi : hi + HALF] = pbuf[3 + 2 * way, t, hi : hi + HALF].astype(bf16)
                rs_copy(it, way, 4, t).start()
            return carry

        lax.fori_loop(0, 4, early, 0)
        for r in (2, 6, 1, 7, 0):
            couple(r)

    def rs_step(it, step):
        rel = (4 - step, 4 + step)

        def one(t, carry):
            for way in range(2):
                rs_copy(it, way, step - 1, t).wait_recv()
                if step == 1:
                    lo = way * HALF
                    rs_s[it, way, 1, t, lo : lo + HALF] = (
                        pbuf[rel[way], t, lo : lo + HALF] + rs_r[it, way, 0, t, lo : lo + HALF].astype(f32)
                    ).astype(bf16)
                else:
                    if step == 2:
                        rs_copy(it, way, 4, t).wait_recv()
                    rs_s[it, way, step, t] = (
                        pbuf[rel[way], t] + rs_r[it, way, step - 1, t].astype(f32)
                    ).astype(bf16)
                rs_copy(it, way, step, t).start()
            return carry

        lax.fori_loop(0, 4, one, 0)

    def rs_end(it, t):
        for way in range(2):
            rs_copy(it, way, 3, t).wait_recv()
        return pbuf[0, t] + (rs_r[it, 0, 3, t].astype(f32) + rs_r[it, 1, 3, t].astype(f32))

    def fold(it, row, value):
        line = jnp.sum(value, axis=0, keepdims=True)
        redv[it, row : row + 1, :] += line[:, :128] + line[:, 128:]

    def ra_copy(it, q, slot):
        return remote(redv.at[it], red_a.at[it, slot], sem_ra.at[it, 0, q], sem_ra.at[it, 1, slot], (pa, q))

    def rb_copy(it, p, slot):
        return remote(redt.at[it], red_b.at[it, slot], sem_rb.at[it, 0, p], sem_rb.at[it, 1, slot], peer(p))

    def reduce_first(it):
        red_a[it, z] = redv[it]
        for q in zs:
            ra_copy(it, q, z).start()

    def reduce_second(it):
        for q in zs:
            ra_copy(it, q, q).wait_recv()
        total = red_a[it, 0]
        for i in range(1, 8):
            total = total + red_a[it, i]
        return total

    def reduce_peers(it, total):
        redt[it] = total
        red_b[it, j] = total
        for p in peers:
            rb_copy(it, p, j).start()

    def reduce_last(it):
        for p in peers:
            rb_copy(it, p, p).wait_recv()
        return finish([red_b[it, i] for i in range(8)])

    def rc_copy(q, slot):
        return remote(redt.at[1], red_c.at[slot], sem_rc.at[0, q], sem_rc.at[1, slot], (q, z))

    def finish(tiles):
        total = tiles[0]
        for tile in tiles[1:]:
            total = total + tile
        sums = jnp.sum(total, axis=1, keepdims=True)
        qw, ss, sq, qq = sums[0:1], sums[1:2], sums[2:3], sums[3:4]
        alpha = qw / CELLS
        rest = 1.0 - alpha
        squares = ss + 2.0 * rest * sq + rest * rest * qq
        beta = jnp.sqrt(jnp.maximum(squares, 0.0) / CELLS + EPS)
        return alpha, rest, beta

    redv[...] = jnp.zeros_like(redv)
    ag_first(0, tme)
    for d in (2, 1, 0):
        x_copy(d, others[d]).wait_recv()
        ag_first(0, others[d])
    for load in loads[2:5]:
        load.wait()
    spread_edges(offset_raw, tile_raw, term_raw, count_raw, meta_in, X, g)
    build(tme)
    order = [tme] + others[::-1]
    for t in order:
        ag_second(0, t)
    loads[5].wait()
    split_energies(q0_raw, q0_in)
    spread_propagator(prop_raw, square, prop_in)
    q1g[tme] = q1_in[e]
    q0g[tme] = q0_in[e]
    pg[tme] = prop_in[e]
    for d in (2, 1, 0):
        in_copy(0, d, others[d]).wait_recv()
        build(others[d])
    for t in range(4):
        ag_last(0, t)
        spline_step(0, t, t == 0, t == 3)
    coupling_copy.wait()
    rs_begin(0)
    for kind in (1, 2, 3):
        for d in range(3):
            in_copy(kind, d, tme).start()
    for step in (1, 2, 3):
        rs_step(0, step)
    for kind in (1, 2, 3):
        for d in range(3):
            in_copy(kind, d, others[d]).wait_recv()
    beta0 = beta_in[e]

    def first_end(t):
        y = rs_end(0, t)
        y1g[t] = y
        q1 = q1g[t]
        pw = jnp.concatenate([pg[t], pg[t]], axis=1) * y
        s = -pw - beta0 * q0g[t]
        sg[t] = s
        xg[1, t, j] = s.astype(bf16)
        ag_first(1, t)
        fold(0, 0, q1 * (q1 - pw))
        fold(0, 1, s * s)
        fold(0, 2, s * q1)
        fold(0, 3, q1 * q1)

    for t in range(4):
        first_end(t)
    ag_second(1, 0)
    reduce_first(0)
    ag_second(1, 1)

    ag_second(1, 2)
    ag_second(1, 3)
    ag_last(1, 0)
    spline_step(1, 0, True, False)
    reduce_peers(0, reduce_second(0))
    for t in range(1, 4):
        ag_last(1, t)
        spline_step(1, t, False, t == 3)
    rs_begin(1)
    rs_step(1, 1)
    alpha1, rest1, beta1 = reduce_last(0)

    def fin_copy(kind, d, slot):
        t = others[d]
        src = (q2g.at[t], s2g.at[t])[kind]
        dst = (fin_q, fin_s)[kind].at[slot]
        return remote(src, dst, sem_fin.at[0, kind, d], sem_fin.at[1, kind, slot], member(t))

    for t in range(4):
        q2g[t] = (sg[t] + rest1 * q1g[t]) / beta1
    fin_q[e] = q2g[tme]
    for d in range(3):
        fin_copy(0, d, e).start()
    rs_step(1, 2)
    rs_step(1, 3)
    for t in range(4):
        y = (rs_end(1, t) + rest1 * y1g[t]) / beta1
        q2 = q2g[t]
        pw = jnp.concatenate([pg[t], pg[t]], axis=1) * y
        s = -pw - beta1 * q1g[t]
        s2g[t] = s
        fold(1, 0, q2 * (q2 - pw))
        fold(1, 1, s * s)
        fold(1, 2, s * q2)
        fold(1, 3, q2 * q2)
    reduce_first(1)
    fin_s[e] = s2g[tme]
    for d in range(3):
        fin_copy(1, d, e).start()
    total = reduce_second(1)
    wide = lambda v: jnp.broadcast_to(v, (1, 128))
    total = jnp.concatenate([total[0:4], wide(alpha1), wide(beta1), total[6:8]], axis=0)
    redt[1] = total
    red_c[pa] = total
    for q in plane:
        rc_copy(q, pa).start()
    for kind in range(2):
        for d in range(3):
            fin_copy(kind, d, energy_of(others[d], g)).wait_recv()
        for q in range(4):
            (q1_raw, q0_raw)[kind][:, :, q, :] = (fin_q, fin_s)[kind][q].reshape(2, HALF, CH)
    for q in plane:
        rc_copy(q, q).wait_recv()
    lanes = lax.broadcasted_iota(jnp.int32, (1, 128), 1)
    lines = [jnp.zeros((1, 128), f32)] * 4
    rests, scales = [], []
    for q in range(4):
        tiles = [red_c[i] for i in range(32) if owned(i) == q]
        alpha2, rest2, beta2 = finish(tiles)
        rests.append(rest2)
        scales.append(1.0 / beta2)
        found = (tiles[0][4:5], tiles[0][5:6], wide(alpha2), wide(beta2))
        lines = [jnp.where(lanes == q, new, old) for new, old in zip(found, lines)]
    coef[...] = jnp.concatenate(lines, axis=0)[:, :4]
    column = lambda v: jnp.broadcast_to(jnp.concatenate(v, axis=0), (4, CH))[None, None]
    out[...] = (q0_raw[...] + column(rests) * q1_raw[...]) * column(scales)

    for d in range(3):
        x_copy(d, tme).wait_send()
        for kind in range(4):
            in_copy(kind, d, tme).wait_send()
        for kind in range(2):
            fin_copy(kind, d, e).wait_send()
    for it in range(2):

        def drain(t, carry):
            for k in range(9):
                ag_send(it, t, k).wait_send()
            for way in range(2):
                for step in range(5):
                    rs_copy(it, way, step, t).wait_send()
            return carry

        lax.fori_loop(0, 4, drain, 0)
        for q in zs:
            ra_copy(it, q, z).wait_send()
    for p in peers:
        rb_copy(0, p, j).wait_send()
    for q in plane:
        rc_copy(q, pa).wait_send()


def hand_over(out_in, coef_in, out, coef):
    out[...] = out_in[...]
    coef[...] = coef_in[...]


def body(
    basis_prev,
    basis_now,
    beta_prev,
    propagator,
    spline,
    coupling,
    edge_offset,
    edge_tile,
    edge_term,
    edge_count,
):
    f32 = jnp.float32
    bf16 = jnp.bfloat16
    tiles = spline.transpose(0, 1, 2, 4, 3).reshape(2048, HALF)
    flat = lambda v: v.transpose(0, 2, 1)

    vmem = pl.BlockSpec(memory_space=pltpu.VMEM)
    anywhere = pl.BlockSpec(memory_space=pl.ANY)
    dma = pltpu.SemaphoreType.DMA
    out, coef = pl.pallas_call(
        kernel,
        out_shape=(
            jax.ShapeDtypeStruct((2, HALF, 4, CH), f32),
            jax.ShapeDtypeStruct((4, 4), f32),
        ),
        in_specs=[
            anywhere,
            anywhere,
            pl.BlockSpec(memory_space=pltpu.SMEM),
            vmem,
            anywhere,
            anywhere,
            anywhere,
            anywhere,
            vmem,
            anywhere,
        ],
        out_specs=(vmem, vmem),
        scratch_shapes=[
            pltpu.VMEM((3, 2048, CH), bf16),
            pltpu.VMEM((2, HALF, 4, CH), f32),
            pltpu.VMEM((2, HALF, 4, CH), f32),
            pltpu.VMEM((2048, HALF), bf16),
            pltpu.VMEM((32, 4, 32), jnp.int32),
            pltpu.VMEM((32, 4, 32), jnp.int32),
            pltpu.VMEM((32, 4, 32), jnp.int32),
            pltpu.VMEM((4, ROWS, CH), f32),
            pltpu.VMEM((4, ROWS, CH), f32),
            pltpu.VMEM((4, ROWS, 128), f32),
            pltpu.VMEM((128, 128), f32),
            pltpu.VMEM((8, HALF, CH), bf16),
            pltpu.VMEM((8, 8, CH), jnp.int32),
            pltpu.VMEM((3, ROWS, CH), bf16),
            pltpu.VMEM((4, 8, HALF, CH), bf16),
            pltpu.VMEM((4, 4, 288, 768), bf16),
            pltpu.VMEM((2, 4, 8, ROWS, CH), bf16),
            pltpu.VMEM((4, 288, CH), f32),
            pltpu.VMEM((4, ROWS, 768), bf16),
            pltpu.VMEM((8, 4, ROWS, CH), f32),
            pltpu.VMEM((2, 2, 4, 4, ROWS, CH), bf16),
            pltpu.VMEM((2, 2, 4, 4, ROWS, CH), bf16),
            pltpu.VMEM((4, ROWS, CH), f32),
            pltpu.VMEM((4, ROWS, CH), f32),
            pltpu.VMEM((4, ROWS, 128), f32),
            pltpu.VMEM((4, ROWS, CH), f32),
            pltpu.VMEM((4, ROWS, CH), f32),
            pltpu.VMEM((4, ROWS, CH), f32),
            pltpu.VMEM((4, ROWS, CH), f32),
            pltpu.VMEM((4, ROWS, CH), f32),
            pltpu.VMEM((4, ROWS, CH), f32),
            pltpu.VMEM((2, 8, 128), f32),
            pltpu.VMEM((2, 8, 8, 128), f32),
            pltpu.VMEM((2, 8, 128), f32),
            pltpu.VMEM((2, 8, 8, 128), f32),
            pltpu.VMEM((32, 8, 128), f32),
            dma((2, 4)),
            dma((2, 4, 4)),
            dma((2, 2, 4, 9)),
            dma((2, 2, 2, 5, 4)),
            dma((2, 2, 8)),
            dma((2, 2, 8)),
            dma((2, 32)),
            dma((2, 2, 4)),
            dma(()),
            dma((6,)),
        ],
        compiler_params=pltpu.CompilerParams(
            collective_id=0, has_side_effects=True, vmem_limit_bytes=56 * 1024 * 1024
        ),
    )(
        basis_now,
        basis_prev,
        beta_prev,
        flat(propagator),
        tiles,
        flat(edge_offset),
        flat(edge_tile),
        flat(edge_term),
        edge_count,
        coupling,
    )
    shapes = (jax.ShapeDtypeStruct((2, HALF, 4, CH), f32), jax.ShapeDtypeStruct((4, 4), f32))
    return pl.pallas_call(
        hand_over,
        out_shape=shapes,
        in_specs=[vmem] * 2,
        out_specs=(vmem, vmem),
    )(out, coef)


def solution(mesh):
    placed = (
        P("pa", None, None, "ch"),
        P("pa", None, None, "ch"),
        P(),
        P("pa", None, None),
        P(None, "pa", None, None, None),
        P(None, None, "ch"),
        P(),
        P(),
        P(),
        P(),
    )
    return jax.shard_map(
        body,
        mesh=mesh,
        in_specs=placed,
        out_specs=(P("pa", None, None, "ch"), P()),
        check_vma=False,
    )
```
